256 devices in a mesh: orb: 8 (over x, z_hi), gx: 4 (over y), gy: 8 (over z_lo, core).
Axes of the slice: x: 4, y: 4, z: 8 (z_hi: 2, z_lo: 4; z = z_hi * 4 + z_lo), core: 2. Of those that a mesh axis runs over, the one named last changes fastest.
Arguments:
- orbitals: float32 [16, 48, 128, 512], P('orb', None, 'gy', 'gx'), may hold values from 1 to 2
- potential: float32 [48, 128, 512], P(None, 'gy', 'gx'), may hold values from 0 to 0.5
- cheb_coeffs: float32 [4], replicated, may hold values from 0.1 to 1, as said below
Outputs:
- density: float32 [48, 128, 512], P('orb', 'gy', 'gx')
The draws below stay inside these ranges and needn't reach their ends.
Inputs may be any that keep to these rules, and one draw needn't show every extreme that they name: `cheb_coeffs`: 4 weights; the last one is 0.7 or more, the others 0.3 or less.
All inputs are finite; a program needn't handle non-finite values.
Results may differ from the reference program's by a relative error of at most 0.00002.
Values sent between devices are 32-bit elements; how exact they have to be, the bound alone decides.
A program may use at most 128 MiB of HBM per device.

```python
import jax
import jax.numpy as jnp
from jax import lax

NZ = 48
CHEB = 3
NX = 512
NY = 128
ORBITALS = 16


def draw_cheb_coeffs(key, part):
    lower_key, upper_key = jax.random.split(jax.random.fold_in(key, 7))
    lower_terms = jax.random.uniform(lower_key, (CHEB,), jnp.float32, 0.1, 0.3)
    upper_term = jax.random.uniform(upper_key, (1,), jnp.float32, 0.7, 1.0)
    return jnp.concatenate([lower_terms, upper_term], 0)


def levels(key, shape, cuts, least, high):
    def one(dim, blocks):
        steps = jax.random.uniform(jax.random.fold_in(jax.random.fold_in(key, 6), dim), (blocks,), jnp.float32, least / len(cuts), high / len(cuts))
        return jnp.repeat(jnp.exp(steps), shape[dim] // blocks).reshape((-1,) + (1,) * (len(shape) - dim - 1))

    gain = one(*cuts[0])
    for cut in cuts[1:]:
        gain = gain * one(*cut)
    return gain


def setup_inputs(seed: int = 0) -> dict:
    key_list = jax.random.split(jax.random.key(seed), 4)
    return {
        "orbitals": jnp.clip(1.0 + 1.0 * jax.random.uniform(key_list[0], (ORBITALS, NZ, NY, NX), jnp.float32) ** levels(key_list[0], (ORBITALS, NZ, NY, NX), ((0, 8), (2, 8), (3, 4)), -0.2, 0.2), 1.0, 2.0),
        "potential": jnp.clip(0.5 * jax.random.uniform(key_list[1], (NZ, NY, NX), jnp.float32) ** levels(key_list[1], (NZ, NY, NX), ((1, 8), (2, 4)), -0.2, 0.2), 0.0, 0.5),
        "cheb_coeffs": draw_cheb_coeffs(jax.random.fold_in(key_list[3], 71), 0),
    }


STENCIL_COEFFS = (-205.0 / 72.0, 8.0 / 5.0, -1.0 / 5.0, 8.0 / 315.0, -1.0 / 560.0)
ENERGY_SHIFT = 5.875
ENERGY_SPREAD = 6.0


def laplace(values):
    summed = 3.0 * STENCIL_COEFFS[0] * values
    for offset in range(1, 5):
        for axis_index in range(3):
            summed = summed + STENCIL_COEFFS[offset] * (jnp.roll(values, offset, axis_index) + jnp.roll(values, -offset, axis_index))
    return summed


def reference(orbitals, potential, cheb_coeffs):
    def hamiltonian(values):
        return (-0.5 * laplace(values) + (potential - ENERGY_SHIFT) * values) / ENERGY_SPREAD

    def filter_orbital(carry, orbital):
        previous = orbital
        current = hamiltonian(orbital)
        filtered = cheb_coeffs[0] * orbital + cheb_coeffs[1] * current
        for step in range(1, CHEB):
            following = 2.0 * hamiltonian(current) - previous
            filtered = filtered + cheb_coeffs[step + 1] * following
            previous, current = current, following
        return carry + filtered * filtered, None

    start = jnp.zeros(potential.shape, jnp.float32)
    squares, unused = lax.scan(filter_orbital, start, orbitals)
    return squares / ORBITALS
```

```python
import jax
import jax.numpy as jnp
from jax import lax
from jax.experimental import pallas as pl
from jax.experimental.pallas import tpu as pltpu
from jax.sharding import PartitionSpec as P

MESH = pl.DeviceIdType.MESH

CHEB = 3
STENCIL = (-205.0 / 72.0, 8.0 / 5.0, -1.0 / 5.0, 8.0 / 315.0, -1.0 / 560.0)
WHOLE = (0.0, 8064.0, -1008.0, 128.0, -9.0)
SHIFT = 5.875
SPREAD = 6.0
LAP = tuple(-0.5 * s / SPREAD for s in STENCIL)
MXU_SCALE = -0.5 / SPREAD / 5040.0

NZ = 48
NORB = 2
ROWS = 16
LANES = 128
CHUNKS = 8
PLANES = NZ // CHUNKS
TILES = PLANES * NORB
TOP = 8


def split_bf16(values):
    high = values.astype(jnp.bfloat16)
    low = (values - high.astype(jnp.float32)).astype(jnp.bfloat16)
    return jnp.concatenate([high, low], axis=1)


def band_weights():
    row = lax.rem(lax.broadcasted_iota(jnp.int32, (2 * LANES, LANES), 0), LANES)
    column = lax.broadcasted_iota(jnp.int32, (2 * LANES, LANES), 1)
    distance = jnp.abs(row - column)
    weights = jnp.zeros((2 * LANES, LANES), jnp.float32)
    for j in range(1, 5):
        weights = jnp.where(distance == j, WHOLE[j], weights)
    return weights.astype(jnp.bfloat16)


def edge_weights():
    row = lax.rem(lax.broadcasted_iota(jnp.int32, (2 * LANES, LANES), 0), LANES)
    column = lax.broadcasted_iota(jnp.int32, (2 * LANES, LANES), 1)
    distance = jnp.abs(row - column)
    crosses = (row // 8 == column // 8) & (row // 4 != column // 4)
    weights = jnp.zeros((2 * LANES, LANES), jnp.float32)
    for j in range(1, 5):
        weights = jnp.where(crosses & (distance == j), WHOLE[j], weights)
    return weights.astype(jnp.bfloat16)


def kernel(
    orbitals, potential, coeffs, out,
    t0, t1, t2, acc, pot, band, edge, packed, beside, squares, arrived, forward, other,
    local_sem, y_send, y_recv, x_send, x_recv, q_send, q_recv, z_send, z_recv,
):
    terms = (t0, t1, t2)
    orb, gx, gy = lax.axis_index("orb"), lax.axis_index("gx"), lax.axis_index("gy")
    n_gx, n_gy = lax.axis_size("gx"), lax.axis_size("gy")
    ox, oz = orb // 2, lax.rem(orb, 2)

    def chunk_at(position):
        to_x = lax.rem(ox + 1 + position, 4)
        to_z = lax.rem(oz + 1 + position // 4, 2)
        return to_x * 2 + to_z

    up, down = {"gy": lax.rem(gy + 1, n_gy)}, {"gy": lax.rem(gy + n_gy - 1, n_gy)}
    right, left = {"gx": lax.rem(gx + 1, n_gx)}, {"gx": lax.rem(gx + n_gx - 1, n_gx)}

    def along_x(distance):
        return {"orb": lax.rem(ox + distance, 4) * 2 + oz}

    across = {"orb": ox * 2 + 1 - oz}

    loads = [
        pltpu.make_async_copy(
            orbitals.at[o], t0.at[:, o, pl.ds(TOP, ROWS)], local_sem.at[o]
        )
        for o in range(NORB)
    ]
    loads.append(pltpu.make_async_copy(potential, pot, local_sem.at[NORB]))
    for load in loads:
        load.start()

    barrier = pltpu.get_barrier_semaphore()
    partners = [up, down, right, left, along_x(1), along_x(2), along_x(3), across]
    for partner in partners:
        pl.semaphore_signal(barrier, inc=1, device_id=partner, device_id_type=MESH)

    def y_copy(k, planes, position, way):
        term = terms[k]
        source, target = (TOP + ROWS - 4, TOP - 4) if way == 0 else (TOP, TOP + ROWS)
        return pltpu.make_async_remote_copy(
            src_ref=term.at[planes, :, pl.ds(source, 4)],
            dst_ref=term.at[planes, :, pl.ds(target, 4)],
            send_sem=y_send.at[k, way],
            recv_sem=y_recv.at[k, position, way],
            device_id=up if way == 0 else down,
            device_id_type=MESH,
        )

    def x_copy(k, position, way):
        return pltpu.make_async_remote_copy(
            src_ref=packed.at[k, position],
            dst_ref=beside.at[k, way, position],
            send_sem=x_send.at[k, way],
            recv_sem=x_recv.at[k, position, way],
            device_id=right if way == 0 else left,
            device_id_type=MESH,
        )

    def chunk_planes(position):
        return pl.ds(chunk_at(position) * PLANES, PLANES)

    def send_edges(k, position):
        planes = chunk_planes(position)
        for way in range(2):
            y_copy(k, planes, position, way).start()
        for way in range(2):
            x_copy(k, position, way).start()

    lane = lax.broadcasted_iota(jnp.int32, (ROWS, LANES), 1)
    at_edge = (lane < 4) | (lane >= LANES - 4)

    def pack(tiles):
        result = jnp.zeros((ROWS, LANES), jnp.float32)
        for g, tile in enumerate(tiles):
            result = jnp.where(lane // 8 == g, pltpu.roll(tile, 8 * g + 4, 1), result)
        return result

    band[...] = band_weights()
    edge[...] = edge_weights()
    for load in loads:
        load.wait()

    @pl.loop(0, CHUNKS)
    def _(position):
        z = chunk_at(position) * PLANES
        packed[0, position] = pack(
            [t0[z + i, o, pl.ds(TOP, ROWS), :] for i in range(PLANES) for o in range(NORB)]
        )

    pl.semaphore_wait(barrier, len(partners))

    @pl.loop(0, CHUNKS)
    def _(position):
        send_edges(0, position)

    @pl.loop(0, NZ // 4)
    def _(i):
        rows = pl.ds(i * 4, 4)
        pot[rows] = pot[rows] * (1.0 / SPREAD) + (-SHIFT / SPREAD + 3.0 * LAP[0])

    c0, c1, c2, c3 = coeffs[0], coeffs[1], coeffs[2], coeffs[3]

    def inside(k):
        term = terms[k]

        @pl.loop(0, CHUNKS)
        def _(chunk):
            z = chunk * PLANES
            for o in range(NORB):
                planes = [
                    term[lax.rem(z + d + NZ, NZ), o, pl.ds(TOP, ROWS), :]
                    for d in range(-4, PLANES + 4)
                ]
                block = jnp.concatenate(planes[4 : 4 + PLANES], axis=0)
                along = jnp.dot(
                    split_bf16(block), band[...], preferred_element_type=jnp.float32
                )
                for i in range(PLANES):
                    centre = planes[4 + i]
                    total = pot[z + i] * centre + MXU_SCALE * along[ROWS * i : ROWS * (i + 1)]
                    for j in range(1, 5):
                        total = total + LAP[j] * (planes[4 + i - j] + planes[4 + i + j])
                    if k == 0:
                        t1[z + i, o, pl.ds(TOP, ROWS), :] = total
                    elif k == 1:
                        t2[z + i, o, pl.ds(TOP, ROWS), :] = (
                            2.0 * total - t0[z + i, o, pl.ds(TOP, ROWS), :]
                        )
                    else:
                        acc[z + i, o] = (
                            (2.0 * c3) * total
                            + c2 * centre
                            + (c1 - c3) * t1[z + i, o, pl.ds(TOP, ROWS), :]
                            + c0 * t0[z + i, o, pl.ds(TOP, ROWS), :]
                        )

    def across_edges(k, position):
        term = terms[k]
        z = chunk_at(position) * PLANES
        for way in range(2):
            x_copy(k, position, way).wait_recv()
        side = jnp.where(
            lax.rem(lane, 8) < 4, beside[k, 0, position], beside[k, 1, position]
        )
        sides = MXU_SCALE * jnp.dot(
            split_bf16(side), edge[...], preferred_element_type=jnp.float32
        )
        for way in range(2):
            y_copy(k, chunk_planes(position), position, way).wait_recv()
        totals = []
        for i in range(PLANES):
            for o in range(NORB):
                g = i * NORB + o
                total = jnp.where(at_edge, pltpu.roll(sides, LANES - 4 - 8 * g, 1), 0.0)
                for j in range(1, 5):
                    total = total + LAP[j] * (
                        term[z + i, o, pl.ds(TOP - j, ROWS), :]
                        + term[z + i, o, pl.ds(TOP + j, ROWS), :]
                    )
                totals.append(total)
        return z, totals

    for k in range(CHEB - 1):
        inside(k)
        following = terms[k + 1]

        @pl.loop(0, CHUNKS)
        def _(position):
            z, totals = across_edges(k, position)
            tiles = []
            for i in range(PLANES):
                for o in range(NORB):
                    total = totals[i * NORB + o]
                    if k > 0:
                        total = 2.0 * total
                    tile = following[z + i, o, pl.ds(TOP, ROWS), :] + total
                    following[z + i, o, pl.ds(TOP, ROWS), :] = tile
                    tiles.append(tile)
            packed[k + 1, position] = pack(tiles)
            send_edges(k + 1, position)

    def q_copy(position):
        distance = lax.rem(position, 4)
        return pltpu.make_async_remote_copy(
            src_ref=squares.at[position],
            dst_ref=arrived.at[position],
            send_sem=q_send.at[position],
            recv_sem=q_recv.at[position],
            device_id=along_x(distance + 1),
            device_id_type=MESH,
        )

    inside(CHEB - 1)

    @pl.loop(0, CHUNKS)
    def _(position):
        z, totals = across_edges(CHEB - 1, position)
        for i in range(PLANES):
            total = None
            for o in range(NORB):
                value = acc[z + i, o] + (2.0 * c3) * totals[i * NORB + o]
                total = value * value if total is None else total + value * value
            squares[position, i] = total

        @pl.when(lax.rem(position, 4) != 3)
        def _():
            q_copy(position).start()

    for position in range(3):
        q_copy(position).wait_recv()
    forward[...] = (squares[3] + arrived[0]) + (arrived[1] + arrived[2])
    to_owner = pltpu.make_async_remote_copy(
        src_ref=forward, dst_ref=other, send_sem=z_send.at[0], recv_sem=z_recv.at[0],
        device_id=across, device_id_type=MESH,
    )
    to_owner.start()

    for k in range(CHEB):
        for way in range(2):
            pltpu.make_async_remote_copy(
                src_ref=packed.at[k],
                dst_ref=beside.at[k, way],
                send_sem=x_send.at[k, way],
                recv_sem=x_recv.at[k, 0, way],
                device_id=right if way == 0 else left,
                device_id_type=MESH,
            ).wait_send()
            y_copy(k, pl.ds(0, NZ), 0, way).wait_send()
    for position in (0, 1, 2, 4, 5, 6):
        q_copy(position).wait_send()

    for position in range(4, 7):
        q_copy(position).wait_recv()
    mine = (squares[7] + arrived[4]) + (arrived[5] + arrived[6])
    to_owner.wait()
    out[...] = (mine + other[...]) * (1.0 / 16.0)


def local(orbitals, potential, coeffs):
    return pl.pallas_call(
        kernel,
        out_shape=jax.ShapeDtypeStruct((PLANES, ROWS, LANES), jnp.float32),
        in_specs=[
            pl.BlockSpec(memory_space=pl.ANY),
            pl.BlockSpec(memory_space=pl.ANY),
            pl.BlockSpec(memory_space=pltpu.SMEM),
        ],
        out_specs=pl.BlockSpec(memory_space=pltpu.VMEM),
        scratch_shapes=[
            pltpu.VMEM((NZ, NORB, 32, LANES), jnp.float32),
            pltpu.VMEM((NZ, NORB, 32, LANES), jnp.float32),
            pltpu.VMEM((NZ, NORB, 32, LANES), jnp.float32),
            pltpu.VMEM((NZ, NORB, ROWS, LANES), jnp.float32),
            pltpu.VMEM((NZ, ROWS, LANES), jnp.float32),
            pltpu.VMEM((2 * LANES, LANES), jnp.bfloat16),
            pltpu.VMEM((2 * LANES, LANES), jnp.bfloat16),
            pltpu.VMEM((CHEB, CHUNKS, ROWS, LANES), jnp.float32),
            pltpu.VMEM((CHEB, 2, CHUNKS, ROWS, LANES), jnp.float32),
            pltpu.VMEM((CHUNKS, PLANES, ROWS, LANES), jnp.float32),
            pltpu.VMEM((CHUNKS, PLANES, ROWS, LANES), jnp.float32),
            pltpu.VMEM((PLANES, ROWS, LANES), jnp.float32),
            pltpu.VMEM((PLANES, ROWS, LANES), jnp.float32),
            pltpu.SemaphoreType.DMA((NORB + 1,)),
            pltpu.SemaphoreType.DMA((CHEB, 2)),
            pltpu.SemaphoreType.DMA((CHEB, CHUNKS, 2)),
            pltpu.SemaphoreType.DMA((CHEB, 2)),
            pltpu.SemaphoreType.DMA((CHEB, CHUNKS, 2)),
            pltpu.SemaphoreType.DMA((CHUNKS,)),
            pltpu.SemaphoreType.DMA((CHUNKS,)),
            pltpu.SemaphoreType.DMA((1,)),
            pltpu.SemaphoreType.DMA((1,)),
        ],
        compiler_params=pltpu.CompilerParams(
            collective_id=0, has_side_effects=True, vmem_limit_bytes=48 * 2**20
        ),
        name="chebyshev",
    )(orbitals, potential, coeffs)


def solution(mesh):
    in_specs = (P("orb", None, "gy", "gx"), P(None, "gy", "gx"), P())
    out_specs = P("orb", "gy", "gx")
    return jax.shard_map(local, mesh=mesh, in_specs=in_specs, out_specs=out_specs, check_vma=False)
```

```python
import jax
import jax.numpy as jnp
from jax import lax
from jax.experimental import pallas as pl
from jax.experimental.pallas import tpu as pltpu
from jax.sharding import PartitionSpec as P

MESH = pl.DeviceIdType.MESH

CHEB = 3
STENCIL = (-205.0 / 72.0, 8.0 / 5.0, -1.0 / 5.0, 8.0 / 315.0, -1.0 / 560.0)
WHOLE = (0.0, 8064.0, -1008.0, 128.0, -9.0)
SHIFT = 5.875
SPREAD = 6.0
LAP = tuple(-0.5 * s / SPREAD for s in STENCIL)
MXU_SCALE = -0.5 / SPREAD / 5040.0

NZ = 48
NORB = 2
ROWS = 16
LANES = 128
CHUNKS = 8
PLANES = NZ // CHUNKS
TILES = PLANES * NORB
SPAN = 12
BATCH = 4
GROUP = 2
TOP = 8


def split_bf16(values):
    high = values.astype(jnp.bfloat16)
    low = (values - high.astype(jnp.float32)).astype(jnp.bfloat16)
    return jnp.concatenate([high, low], axis=1)


def band_weights():
    row = lax.rem(lax.broadcasted_iota(jnp.int32, (2 * LANES, LANES), 0), LANES)
    column = lax.broadcasted_iota(jnp.int32, (2 * LANES, LANES), 1)
    distance = jnp.abs(row - column)
    weights = jnp.zeros((2 * LANES, LANES), jnp.float32)
    for j in range(1, 5):
        weights = jnp.where(distance == j, WHOLE[j], weights)
    return weights.astype(jnp.bfloat16)


def edge_weights():
    row = lax.rem(lax.broadcasted_iota(jnp.int32, (2 * LANES, LANES), 0), LANES)
    column = lax.broadcasted_iota(jnp.int32, (2 * LANES, LANES), 1)
    distance = jnp.abs(row - column)
    crosses = (row // 8 == column // 8) & (row // 4 != column // 4)
    weights = jnp.zeros((2 * LANES, LANES), jnp.float32)
    for j in range(1, 5):
        weights = jnp.where(crosses & (distance == j), WHOLE[j], weights)
    return weights.astype(jnp.bfloat16)


def kernel(
    orbitals, potential, coeffs, out,
    t0, t1, t2, acc, pot, band, edge, packed, beside, squares, arrived, forward, other,
    small, local_sem, y_send, y_recv, x_send, x_recv, q_send, q_recv, z_send, z_recv,
):
    terms = (t0, t1, t2)
    orb, gx, gy = lax.axis_index("orb"), lax.axis_index("gx"), lax.axis_index("gy")
    n_gx, n_gy = lax.axis_size("gx"), lax.axis_size("gy")
    ox, oz = orb // 2, lax.rem(orb, 2)

    def chunk_at(position):
        to_x = lax.rem(ox + 1 + position, 4)
        to_z = lax.rem(oz + 1 + position // 4, 2)
        return to_x * 2 + to_z

    up, down = {"gy": lax.rem(gy + 1, n_gy)}, {"gy": lax.rem(gy + n_gy - 1, n_gy)}
    right, left = {"gx": lax.rem(gx + 1, n_gx)}, {"gx": lax.rem(gx + n_gx - 1, n_gx)}

    def along_x(distance):
        return {"orb": lax.rem(ox + distance, 4) * 2 + oz}

    across = {"orb": ox * 2 + 1 - oz}

    loads = [
        pltpu.make_async_copy(
            orbitals.at[o], t0.at[:, o, pl.ds(TOP, ROWS)], local_sem.at[o]
        )
        for o in range(NORB)
    ]
    loads.append(pltpu.make_async_copy(potential, pot, local_sem.at[NORB]))
    loads.append(pltpu.make_async_copy(coeffs, small, local_sem.at[NORB + 1]))
    for load in loads:
        load.start()

    barrier = pltpu.get_barrier_semaphore()
    partners = [up, down, right, left, along_x(1), along_x(2), along_x(3), across]
    for partner in partners:
        pl.semaphore_signal(barrier, inc=1, device_id=partner, device_id_type=MESH)

    def y_copy(k, planes, position, way):
        term = terms[k]
        source, target = (TOP + ROWS - 4, TOP - 4) if way == 0 else (TOP, TOP + ROWS)
        return pltpu.make_async_remote_copy(
            src_ref=term.at[planes, :, pl.ds(source, 4)],
            dst_ref=term.at[planes, :, pl.ds(target, 4)],
            send_sem=y_send.at[k, way],
            recv_sem=y_recv.at[k, position, way],
            device_id=up if way == 0 else down,
            device_id_type=MESH,
        )

    def x_copy(k, position, way):
        return pltpu.make_async_remote_copy(
            src_ref=packed.at[k, position],
            dst_ref=beside.at[k, way, position],
            send_sem=x_send.at[k, way],
            recv_sem=x_recv.at[k, position, way],
            device_id=right if way == 0 else left,
            device_id_type=MESH,
        )

    def chunk_planes(position):
        return pl.ds(chunk_at(position) * PLANES, PLANES)

    def send_edges(k, position):
        planes = chunk_planes(position)
        for way in range(2):
            y_copy(k, planes, position, way).start()
        for way in range(2):
            x_copy(k, position, way).start()

    lane = lax.broadcasted_iota(jnp.int32, (ROWS, LANES), 1)
    in_left = lax.rem(lane, 8) < 4
    at_edge = (lane < 4) | (lane >= LANES - 4)

    group_of = lane // 8

    def pack(tiles):
        result = jnp.zeros((ROWS, LANES), jnp.float32)
        for g, tile in enumerate(tiles):
            result = jnp.where(group_of == g, pltpu.roll(tile, 8 * g + 4, 1), result)
        return result

    band[...] = band_weights()
    edge[...] = edge_weights()
    for load in loads:
        load.wait()

    @pl.loop(0, CHUNKS)
    def _(position):
        z = chunk_at(position) * PLANES
        packed[0, position] = pack(
            [t0[z + i, o, pl.ds(TOP, ROWS), :] for i in range(PLANES) for o in range(NORB)]
        )

    pl.semaphore_wait(barrier, len(partners))

    @pl.loop(0, CHUNKS)
    def _(position):
        send_edges(0, position)

    @pl.loop(0, NZ // 4)
    def _(i):
        rows = pl.ds(i * 4, 4)
        pot[rows] = pot[rows] * (1.0 / SPREAD) + (-SHIFT / SPREAD + 3.0 * LAP[0])

    c0, c1, c2, c3 = small[0], small[1], small[2], small[3]

    def inside(k):
        term = terms[k]

        @pl.loop(0, NZ // SPAN)
        def _(span):
            z = span * SPAN
            block = [term[z + i, o, pl.ds(TOP, ROWS), :] for o in range(NORB) for i in range(SPAN)]
            along = MXU_SCALE * jnp.dot(
                split_bf16(jnp.concatenate(block, axis=0)),
                band[...],
                preferred_element_type=jnp.float32,
            )
            for o in range(NORB):
                for half in range(0, ROWS, 8):
                    rows = pl.ds(TOP + half, 8)
                    planes = [
                        term[lax.rem(z + d + NZ, NZ), o, rows, :] for d in range(-4, SPAN + 4)
                    ]
                    for i in range(SPAN):
                        first = (o * SPAN + i) * ROWS + half
                        centre = planes[4 + i]
                        total = pot[z + i, pl.ds(half, 8)] * centre + along[first : first + 8]
                        for j in range(1, 5):
                            total = total + LAP[j] * (planes[4 + i - j] + planes[4 + i + j])
                        if k == 0:
                            t1[z + i, o, rows, :] = total
                        elif k == 1:
                            t2[z + i, o, rows, :] = 2.0 * total - t0[z + i, o, rows, :]
                        else:
                            acc[z + i, o, pl.ds(half, 8)] = (
                                (2.0 * c3) * total
                                + c2 * centre
                                + (c1 - c3) * t1[z + i, o, rows, :]
                                + c0 * t0[z + i, o, rows, :]
                            )

    def side_terms(k, base):
        blocks = []
        for n in range(BATCH):
            for way in range(2):
                x_copy(k, base + n, way).wait_recv()
            blocks.append(
                jnp.where(in_left, beside[k, 0, base + n], beside[k, 1, base + n])
            )
        return MXU_SCALE * jnp.dot(
            split_bf16(jnp.concatenate(blocks, axis=0)),
            edge[...],
            preferred_element_type=jnp.float32,
        )

    def halo_terms(k, position, sides):
        term = terms[k]
        z = chunk_at(position) * PLANES
        totals = []
        for i in range(PLANES):
            for o in range(NORB):
                g = i * NORB + o
                total = jnp.where(at_edge, pltpu.roll(sides, LANES - 4 - 8 * g, 1), 0.0)
                for j in range(1, 5):
                    total = total + LAP[j] * (
                        term[z + i, o, pl.ds(TOP - j, ROWS), :]
                        + term[z + i, o, pl.ds(TOP + j, ROWS), :]
                    )
                totals.append(total)
        return z, totals

    def by_batches(k, finish, send):
        @pl.loop(0, CHUNKS // BATCH)
        def _(batch):
            base = batch * BATCH
            sides = side_terms(k, base)
            for first in range(0, BATCH, GROUP):
                group = range(first, first + GROUP)
                for n in group:
                    for way in range(2):
                        y_copy(k, chunk_planes(base + n), base + n, way).wait_recv()
                for n in group:
                    finish(base + n, *halo_terms(k, base + n, sides[ROWS * n : ROWS * (n + 1)]))
                for n in group:
                    send(base + n, n)

    for k in range(CHEB - 1):
        inside(k)

        def finish(position, z, totals, k=k):
            following = terms[k + 1]
            tiles = []
            for i in range(PLANES):
                for o in range(NORB):
                    total = totals[i * NORB + o]
                    if k > 0:
                        total = 2.0 * total
                    tile = following[z + i, o, pl.ds(TOP, ROWS), :] + total
                    following[z + i, o, pl.ds(TOP, ROWS), :] = tile
                    tiles.append(tile)
            packed[k + 1, position] = pack(tiles)

        def send(position, n, k=k):
            send_edges(k + 1, position)

        by_batches(k, finish, send)

    def q_copy(position):
        distance = lax.rem(position, 4)
        return pltpu.make_async_remote_copy(
            src_ref=squares.at[position],
            dst_ref=arrived.at[position],
            send_sem=q_send.at[position],
            recv_sem=q_recv.at[position],
            device_id=along_x(distance + 1),
            device_id_type=MESH,
        )

    inside(CHEB - 1)

    def finish(position, z, totals):
        for i in range(PLANES):
            total = None
            for o in range(NORB):
                value = acc[z + i, o] + (2.0 * c3) * totals[i * NORB + o]
                total = value * value if total is None else total + value * value
            squares[position, i] = total

    def send(position, n):
        if n % 4 != 3:
            q_copy(position).start()

    by_batches(CHEB - 1, finish, send)

    for position in range(3):
        q_copy(position).wait_recv()
    forward[...] = (squares[3] + arrived[0]) + (arrived[1] + arrived[2])
    to_owner = pltpu.make_async_remote_copy(
        src_ref=forward, dst_ref=other, send_sem=z_send.at[0], recv_sem=z_recv.at[0],
        device_id=across, device_id_type=MESH,
    )
    to_owner.start()

    for k in range(CHEB):
        for way in range(2):
            pltpu.make_async_remote_copy(
                src_ref=packed.at[k],
                dst_ref=beside.at[k, way],
                send_sem=x_send.at[k, way],
                recv_sem=x_recv.at[k, 0, way],
                device_id=right if way == 0 else left,
                device_id_type=MESH,
            ).wait_send()
            y_copy(k, pl.ds(0, NZ), 0, way).wait_send()
    for position in (0, 1, 2, 4, 5, 6):
        q_copy(position).wait_send()

    for position in range(4, 7):
        q_copy(position).wait_recv()
    mine = (squares[7] + arrived[4]) + (arrived[5] + arrived[6])
    to_owner.wait()
    out[...] = (mine + other[...]) * (1.0 / 16.0)


def local(orbitals, potential, coeffs):
    return pl.pallas_call(
        kernel,
        out_shape=jax.ShapeDtypeStruct((PLANES, ROWS, LANES), jnp.float32),
        in_specs=[
            pl.BlockSpec(memory_space=pl.ANY),
            pl.BlockSpec(memory_space=pl.ANY),
            pl.BlockSpec(memory_space=pl.ANY),
        ],
        out_specs=pl.BlockSpec(memory_space=pltpu.VMEM),
        scratch_shapes=[
            pltpu.VMEM((NZ, NORB, 32, LANES), jnp.float32),
            pltpu.VMEM((NZ, NORB, 32, LANES), jnp.float32),
            pltpu.VMEM((NZ, NORB, 32, LANES), jnp.float32),
            pltpu.VMEM((NZ, NORB, ROWS, LANES), jnp.float32),
            pltpu.VMEM((NZ, ROWS, LANES), jnp.float32),
            pltpu.VMEM((2 * LANES, LANES), jnp.bfloat16),
            pltpu.VMEM((2 * LANES, LANES), jnp.bfloat16),
            pltpu.VMEM((CHEB, CHUNKS, ROWS, LANES), jnp.float32),
            pltpu.VMEM((CHEB, 2, CHUNKS, ROWS, LANES), jnp.float32),
            pltpu.VMEM((CHUNKS, PLANES, ROWS, LANES), jnp.float32),
            pltpu.VMEM((CHUNKS, PLANES, ROWS, LANES), jnp.float32),
            pltpu.VMEM((PLANES, ROWS, LANES), jnp.float32),
            pltpu.VMEM((PLANES, ROWS, LANES), jnp.float32),
            pltpu.SMEM((4,), jnp.float32),
            pltpu.SemaphoreType.DMA((NORB + 2,)),
            pltpu.SemaphoreType.DMA((CHEB, 2)),
            pltpu.SemaphoreType.DMA((CHEB, CHUNKS, 2)),
            pltpu.SemaphoreType.DMA((CHEB, 2)),
            pltpu.SemaphoreType.DMA((CHEB, CHUNKS, 2)),
            pltpu.SemaphoreType.DMA((CHUNKS,)),
            pltpu.SemaphoreType.DMA((CHUNKS,)),
            pltpu.SemaphoreType.DMA((1,)),
            pltpu.SemaphoreType.DMA((1,)),
        ],
        compiler_params=pltpu.CompilerParams(
            collective_id=0, has_side_effects=True, vmem_limit_bytes=60 * 2**20
        ),
        name="chebyshev",
    )(orbitals, potential, coeffs)


def solution(mesh):
    in_specs = (P("orb", None, "gy", "gx"), P(None, "gy", "gx"), P())
    out_specs = P("orb", "gy", "gx")
    return jax.shard_map(local, mesh=mesh, in_specs=in_specs, out_specs=out_specs, check_vma=False)
```

```python
import jax
import jax.numpy as jnp
from jax import lax
from jax.experimental import pallas as pl
from jax.experimental.pallas import tpu as pltpu
from jax.sharding import PartitionSpec as P

MESH = pl.DeviceIdType.MESH

CHEB = 3
STENCIL = (-205.0 / 72.0, 8.0 / 5.0, -1.0 / 5.0, 8.0 / 315.0, -1.0 / 560.0)
WHOLE = (0.0, 8064.0, -1008.0, 128.0, -9.0)
SHIFT = 5.875
SPREAD = 6.0
LAP = tuple(-0.5 * s / SPREAD for s in STENCIL)
MXU_SCALE = -0.5 / SPREAD / 5040.0

NZ = 48
NORB = 2
ROWS = 16
LANES = 128
CHUNKS = 8
PLANES = NZ // CHUNKS
TILES = PLANES * NORB
SPAN = 12
BATCH = 4
GROUP = 1
TOP = 8


def split_bf16(values):
    high = values.astype(jnp.bfloat16)
    low = (values - high.astype(jnp.float32)).astype(jnp.bfloat16)
    return jnp.concatenate([high, low], axis=1)


def band_weights():
    row = lax.rem(lax.broadcasted_iota(jnp.int32, (2 * LANES, LANES), 0), LANES)
    column = lax.broadcasted_iota(jnp.int32, (2 * LANES, LANES), 1)
    distance = jnp.abs(row - column)
    weights = jnp.zeros((2 * LANES, LANES), jnp.float32)
    for j in range(1, 5):
        weights = jnp.where(distance == j, WHOLE[j], weights)
    return weights.astype(jnp.bfloat16)


def edge_weights():
    row = lax.rem(lax.broadcasted_iota(jnp.int32, (2 * LANES, LANES), 0), LANES)
    column = lax.broadcasted_iota(jnp.int32, (2 * LANES, LANES), 1)
    distance = jnp.abs(row - column)
    crosses = (row // 8 == column // 8) & (row // 4 != column // 4)
    weights = jnp.zeros((2 * LANES, LANES), jnp.float32)
    for j in range(1, 5):
        weights = jnp.where(crosses & (distance == j), WHOLE[j], weights)
    return weights.astype(jnp.bfloat16)


def kernel(
    orbitals, potential, coeffs, out,
    t0, t1, t2, acc, pot, band, edge, packed, beside, squares, arrived, forward, other,
    small, local_sem, y_send, y_recv, x_send, x_recv, q_send, q_recv, z_send, z_recv,
):
    terms = (t0, t1, t2)
    orb, gx, gy = lax.axis_index("orb"), lax.axis_index("gx"), lax.axis_index("gy")
    n_gx, n_gy = lax.axis_size("gx"), lax.axis_size("gy")
    ox, oz = orb // 2, lax.rem(orb, 2)

    def distance_at(position):
        return lax.rem(position + 1, 4)

    def chunk_at(position):
        to_x = lax.rem(ox + distance_at(position), 4)
        to_z = lax.rem(oz + 1 + position // 4, 2)
        return to_x * 2 + to_z

    up, down = {"gy": lax.rem(gy + 1, n_gy)}, {"gy": lax.rem(gy + n_gy - 1, n_gy)}
    right, left = {"gx": lax.rem(gx + 1, n_gx)}, {"gx": lax.rem(gx + n_gx - 1, n_gx)}

    core = lax.rem(gy, 2)

    def at(distance, z, on_core):
        return {"orb": lax.rem(ox + distance, 4) * 2 + z, "gy": gy - core + on_core}

    loads = [
        pltpu.make_async_copy(
            orbitals.at[o], t0.at[:, o, pl.ds(TOP, ROWS)], local_sem.at[o]
        )
        for o in range(NORB)
    ]
    loads.append(pltpu.make_async_copy(potential, pot, local_sem.at[NORB]))
    loads.append(pltpu.make_async_copy(coeffs, small, local_sem.at[NORB + 1]))
    for load in loads:
        load.start()

    barrier = pltpu.get_barrier_semaphore()
    partners = [up, down, right, left]
    for to_core in (core, 1 - core):
        partners += [at(distance, oz, to_core) for distance in (2, 1, 3)]
        partners.append(at(0, 1 - oz, to_core))
    for partner in partners:
        pl.semaphore_signal(barrier, inc=1, device_id=partner, device_id_type=MESH)

    def y_copy(k, planes, position, way):
        term = terms[k]
        source, target = (TOP + ROWS - 4, TOP - 4) if way == 0 else (TOP, TOP + ROWS)
        return pltpu.make_async_remote_copy(
            src_ref=term.at[planes, :, pl.ds(source, 4)],
            dst_ref=term.at[planes, :, pl.ds(target, 4)],
            send_sem=y_send.at[k, way],
            recv_sem=y_recv.at[k, position, way],
            device_id=up if way == 0 else down,
            device_id_type=MESH,
        )

    def x_copy(k, position, way):
        return pltpu.make_async_remote_copy(
            src_ref=packed.at[k, position],
            dst_ref=beside.at[k, way, position],
            send_sem=x_send.at[k, way],
            recv_sem=x_recv.at[k, position, way],
            device_id=right if way == 0 else left,
            device_id_type=MESH,
        )

    def chunk_planes(position):
        return pl.ds(chunk_at(position) * PLANES, PLANES)

    def send_edges(k, position):
        planes = chunk_planes(position)
        for way in range(2):
            y_copy(k, planes, position, way).start()
        for way in range(2):
            x_copy(k, position, way).start()

    lane = lax.broadcasted_iota(jnp.int32, (ROWS, LANES), 1)
    in_left = lax.rem(lane, 8) < 4
    at_edge = (lane < 4) | (lane >= LANES - 4)

    group_of = lane // 8

    def pack(tiles):
        result = jnp.zeros((ROWS, LANES), jnp.float32)
        for g, tile in enumerate(tiles):
            result = jnp.where(group_of == g, pltpu.roll(tile, 8 * g + 4, 1), result)
        return result

    band[...] = band_weights()
    edge[...] = edge_weights()
    for load in loads:
        load.wait()

    @pl.loop(0, CHUNKS)
    def _(position):
        z = chunk_at(position) * PLANES
        packed[0, position] = pack(
            [t0[z + i, o, pl.ds(TOP, ROWS), :] for i in range(PLANES) for o in range(NORB)]
        )

    pl.semaphore_wait(barrier, len(partners))

    @pl.loop(0, CHUNKS)
    def _(position):
        send_edges(0, position)

    @pl.loop(0, NZ // 4)
    def _(i):
        rows = pl.ds(i * 4, 4)
        pot[rows] = pot[rows] * (1.0 / SPREAD) + (-SHIFT / SPREAD + 3.0 * LAP[0])

    c0, c1, c2, c3 = small[0], small[1], small[2], small[3]

    def inside(k):
        term = terms[k]

        @pl.loop(0, NZ // SPAN)
        def _(span):
            z = span * SPAN
            block = [term[z + i, o, pl.ds(TOP, ROWS), :] for o in range(NORB) for i in range(SPAN)]
            along = MXU_SCALE * jnp.dot(
                split_bf16(jnp.concatenate(block, axis=0)),
                band[...],
                preferred_element_type=jnp.float32,
            )
            for o in range(NORB):
                for half in range(0, ROWS, 8):
                    rows = pl.ds(TOP + half, 8)
                    planes = [
                        term[lax.rem(z + d + NZ, NZ), o, rows, :] for d in range(-4, SPAN + 4)
                    ]
                    for i in range(SPAN):
                        first = (o * SPAN + i) * ROWS + half
                        centre = planes[4 + i]
                        total = pot[z + i, pl.ds(half, 8)] * centre + along[first : first + 8]
                        for j in range(1, 5):
                            total = total + LAP[j] * (planes[4 + i - j] + planes[4 + i + j])
                        if k == 0:
                            t1[z + i, o, rows, :] = total
                        elif k == 1:
                            t2[z + i, o, rows, :] = 2.0 * total - t0[z + i, o, rows, :]
                        else:
                            acc[z + i, o, pl.ds(half, 8)] = (
                                (2.0 * c3) * total
                                + c2 * centre
                                + (c1 - c3) * t1[z + i, o, rows, :]
                                + c0 * t0[z + i, o, rows, :]
                            )

    def side_terms(k, base):
        blocks = []
        for n in range(BATCH):
            for way in range(2):
                x_copy(k, base + n, way).wait_recv()
            blocks.append(
                jnp.where(in_left, beside[k, 0, base + n], beside[k, 1, base + n])
            )
        return MXU_SCALE * jnp.dot(
            split_bf16(jnp.concatenate(blocks, axis=0)),
            edge[...],
            preferred_element_type=jnp.float32,
        )

    def halo_terms(k, position, sides):
        term = terms[k]
        z = chunk_at(position) * PLANES
        totals = []
        for i in range(PLANES):
            for o in range(NORB):
                g = i * NORB + o
                total = jnp.where(at_edge, pltpu.roll(sides, LANES - 4 - 8 * g, 1), 0.0)
                for j in range(1, 5):
                    total = total + LAP[j] * (
                        term[z + i, o, pl.ds(TOP - j, ROWS), :]
                        + term[z + i, o, pl.ds(TOP + j, ROWS), :]
                    )
                totals.append(total)
        return z, totals

    def by_batches(k, finish, send):
        @pl.loop(0, CHUNKS // BATCH)
        def _(batch):
            base = batch * BATCH
            sides = side_terms(k, base)
            for first in range(0, BATCH, GROUP):
                group = range(first, first + GROUP)
                for n in group:
                    for way in range(2):
                        y_copy(k, chunk_planes(base + n), base + n, way).wait_recv()
                for n in group:
                    finish(base + n, *halo_terms(k, base + n, sides[ROWS * n : ROWS * (n + 1)]))
                for n in group:
                    send(base + n, n)

    for k in range(CHEB - 1):
        inside(k)

        def finish(position, z, totals, k=k):
            following = terms[k + 1]
            tiles = []
            for i in range(PLANES):
                for o in range(NORB):
                    total = totals[i * NORB + o]
                    if k > 0:
                        total = 2.0 * total
                    tile = following[z + i, o, pl.ds(TOP, ROWS), :] + total
                    following[z + i, o, pl.ds(TOP, ROWS), :] = tile
                    tiles.append(tile)
            packed[k + 1, position] = pack(tiles)

        def send(position, n, k=k):
            send_edges(k + 1, position)

        by_batches(k, finish, send)

    def q_copy(position):
        own = position // 4
        slot = position + 4 * (own + core * (1 - own))
        return pltpu.make_async_remote_copy(
            src_ref=squares.at[position],
            dst_ref=arrived.at[slot],
            send_sem=q_send.at[position],
            recv_sem=q_recv.at[slot],
            device_id=at(distance_at(position), oz, 1 - own * (1 - core)),
            device_id_type=MESH,
        )

    def wait_arrived(slots):
        for slot in slots:
            pltpu.make_async_copy(
                squares.at[0], arrived.at[slot], q_recv.at[slot]
            ).wait()

    def to_owner(on_core):
        return pltpu.make_async_remote_copy(
            src_ref=forward.at[on_core],
            dst_ref=other,
            send_sem=z_send.at[on_core],
            recv_sem=z_recv.at[0],
            device_id=at(0, 1 - oz, on_core),
            device_id_type=MESH,
        )

    inside(CHEB - 1)

    def finish(position, z, totals):
        for i in range(PLANES):
            total = None
            for o in range(NORB):
                value = acc[z + i, o] + (2.0 * c3) * totals[i * NORB + o]
                total = value * value if total is None else total + value * value
            squares[position, i] = total

    def send(position, n):
        if n % 4 != 3:
            q_copy(position).start()
        else:

            @pl.when((position == 3) & (core == 0))
            def _():
                q_copy(position).start()

    by_batches(CHEB - 1, finish, send)

    @pl.when(core == 1)
    def _():
        wait_arrived((4, 5, 6))
        forward[1] = (squares[3] + arrived[4]) + (arrived[5] + arrived[6])
        to_owner(1).start()
        wait_arrived((0, 1, 2, 3))
        forward[0] = (arrived[0] + arrived[1]) + (arrived[2] + arrived[3])
        to_owner(0).start()

    for k in range(CHEB):
        for way in range(2):
            pltpu.make_async_remote_copy(
                src_ref=packed.at[k],
                dst_ref=beside.at[k, way],
                send_sem=x_send.at[k, way],
                recv_sem=x_recv.at[k, 0, way],
                device_id=right if way == 0 else left,
                device_id_type=MESH,
            ).wait_send()
            y_copy(k, pl.ds(0, NZ), 0, way).wait_send()
    for position in (0, 1, 2, 4, 5, 6):
        q_copy(position).wait_send()

    @pl.when(core == 0)
    def _():
        q_copy(3).wait_send()

    wait_arrived((8, 9, 10))
    mine = (squares[7] + arrived[8]) + (arrived[9] + arrived[10])

    @pl.when(core == 1)
    def _():
        for on_core in range(2):
            to_owner(on_core).wait_send()

    to_owner(0).wait_recv()
    out[...] = (mine + other[...]) * (1.0 / 16.0)


def local(orbitals, potential, coeffs):
    return pl.pallas_call(
        kernel,
        out_shape=jax.ShapeDtypeStruct((PLANES, ROWS, LANES), jnp.float32),
        in_specs=[
            pl.BlockSpec(memory_space=pl.ANY),
            pl.BlockSpec(memory_space=pl.ANY),
            pl.BlockSpec(memory_space=pl.ANY),
        ],
        out_specs=pl.BlockSpec(memory_space=pltpu.VMEM),
        scratch_shapes=[
            pltpu.VMEM((NZ, NORB, 32, LANES), jnp.float32),
            pltpu.VMEM((NZ, NORB, 32, LANES), jnp.float32),
            pltpu.VMEM((NZ, NORB, 32, LANES), jnp.float32),
            pltpu.VMEM((NZ, NORB, ROWS, LANES), jnp.float32),
            pltpu.VMEM((NZ, ROWS, LANES), jnp.float32),
            pltpu.VMEM((2 * LANES, LANES), jnp.bfloat16),
            pltpu.VMEM((2 * LANES, LANES), jnp.bfloat16),
            pltpu.VMEM((CHEB, CHUNKS, ROWS, LANES), jnp.float32),
            pltpu.VMEM((CHEB, 2, CHUNKS, ROWS, LANES), jnp.float32),
            pltpu.VMEM((CHUNKS, PLANES, ROWS, LANES), jnp.float32),
            pltpu.VMEM((12, PLANES, ROWS, LANES), jnp.float32),
            pltpu.VMEM((2, PLANES, ROWS, LANES), jnp.float32),
            pltpu.VMEM((PLANES, ROWS, LANES), jnp.float32),
            pltpu.SMEM((4,), jnp.float32),
            pltpu.SemaphoreType.DMA((NORB + 2,)),
            pltpu.SemaphoreType.DMA((CHEB, 2)),
            pltpu.SemaphoreType.DMA((CHEB, CHUNKS, 2)),
            pltpu.SemaphoreType.DMA((CHEB, 2)),
            pltpu.SemaphoreType.DMA((CHEB, CHUNKS, 2)),
            pltpu.SemaphoreType.DMA((CHUNKS,)),
            pltpu.SemaphoreType.DMA((12,)),
            pltpu.SemaphoreType.DMA((2,)),
            pltpu.SemaphoreType.DMA((1,)),
        ],
        compiler_params=pltpu.CompilerParams(
            collective_id=0, has_side_effects=True, vmem_limit_bytes=55000 * 2**10
        ),
        name="chebyshev",
    )(orbitals, potential, coeffs)


def solution(mesh):
    in_specs = (P("orb", None, "gy", "gx"), P(None, "gy", "gx"), P())
    out_specs = P("orb", "gy", "gx")
    return jax.shard_map(local, mesh=mesh, in_specs=in_specs, out_specs=out_specs, check_vma=False)
```

```python
import jax
import jax.numpy as jnp
from jax import lax
from jax.experimental import pallas as pl
from jax.experimental.pallas import tpu as pltpu
from jax.sharding import PartitionSpec as P

MESH = pl.DeviceIdType.MESH

CHEB = 3
STENCIL = (-205.0 / 72.0, 8.0 / 5.0, -1.0 / 5.0, 8.0 / 315.0, -1.0 / 560.0)
WHOLE = (0.0, 8064.0, -1008.0, 128.0, -9.0)
SHIFT = 5.875
SPREAD = 6.0
LAP = tuple(-0.5 * s / SPREAD for s in STENCIL)
MXU_SCALE = -0.5 / SPREAD / 5040.0

NZ = 48
NORB = 2
ROWS = 16
LANES = 128
CHUNKS = 8
PLANES = NZ // CHUNKS
TILES = PLANES * NORB
SPAN = 12
BATCH = 4
GROUP = 1
TOP = 8


def split_bf16(values):
    high = values.astype(jnp.bfloat16)
    low = (values - high.astype(jnp.float32)).astype(jnp.bfloat16)
    return jnp.concatenate([high, low], axis=1)


def band_weights():
    row = lax.rem(lax.broadcasted_iota(jnp.int32, (2 * LANES, LANES), 0), LANES)
    column = lax.broadcasted_iota(jnp.int32, (2 * LANES, LANES), 1)
    distance = jnp.abs(row - column)
    weights = jnp.zeros((2 * LANES, LANES), jnp.float32)
    for j in range(1, 5):
        weights = jnp.where(distance == j, WHOLE[j], weights)
    return weights.astype(jnp.bfloat16)


def edge_weights():
    row = lax.rem(lax.broadcasted_iota(jnp.int32, (2 * LANES, LANES), 0), LANES)
    column = lax.broadcasted_iota(jnp.int32, (2 * LANES, LANES), 1)
    distance = jnp.abs(row - column)
    crosses = (row // 8 == column // 8) & (row // 4 != column // 4)
    weights = jnp.zeros((2 * LANES, LANES), jnp.float32)
    for j in range(1, 5):
        weights = jnp.where(crosses & (distance == j), WHOLE[j], weights)
    return weights.astype(jnp.bfloat16)


def kernel(
    orbitals, potential, coeffs, out,
    t0, t1, t2, acc, pot, band, edge, packed, beside, squares, arrived, forward, other,
    small, local_sem, y_send, y_recv, x_send, x_recv, q_send, q_recv, z_send, z_recv, ready,
):
    terms = (t0, t1, t2)
    orb, gx, gy = lax.axis_index("orb"), lax.axis_index("gx"), lax.axis_index("gy")
    n_gx, n_gy = lax.axis_size("gx"), lax.axis_size("gy")
    ox, oz = orb // 2, lax.rem(orb, 2)

    def distance_at(position):
        step = lax.rem(position, 4)
        return lax.rem(1 + 2 * step - 3 * (step // 2), 4)

    def chunk_at(position):
        to_x = lax.rem(ox + distance_at(position), 4)
        to_z = lax.rem(oz + 1 + position // 4, 2)
        return to_x * 2 + to_z

    up, down = {"gy": lax.rem(gy + 1, n_gy)}, {"gy": lax.rem(gy + n_gy - 1, n_gy)}
    right, left = {"gx": lax.rem(gx + 1, n_gx)}, {"gx": lax.rem(gx + n_gx - 1, n_gx)}

    core = lax.rem(gy, 2)

    def at(distance, z, on_core):
        return {"orb": lax.rem(ox + distance, 4) * 2 + z, "gy": gy - core + on_core}

    barrier = pltpu.get_barrier_semaphore()

    def signal(semaphore, device):
        pl.semaphore_signal(semaphore, inc=1, device_id=device, device_id_type=MESH)

    partners = [up, down, right, left]
    for to_core in (core, 1 - core):
        partners += [at(distance, oz, to_core) for distance in (2, 1, 3)]
    for partner in partners:
        signal(barrier, partner)

    @pl.when(oz == 0)
    def _():
        for to_core in range(2):
            signal(barrier, at(0, 1, to_core))
        signal(barrier, at(2, 1, core))

    loads = [
        pltpu.make_async_copy(
            orbitals.at[o], t0.at[:, o, pl.ds(TOP, ROWS)], local_sem.at[o]
        )
        for o in range(NORB)
    ]
    loads.append(pltpu.make_async_copy(potential, pot, local_sem.at[NORB]))
    loads.append(pltpu.make_async_copy(coeffs, small, local_sem.at[NORB + 1]))
    for load in loads:
        load.start()

    def y_copy(k, planes, position, way):
        term = terms[k]
        source, target = (TOP + ROWS - 4, TOP - 4) if way == 0 else (TOP, TOP + ROWS)
        return pltpu.make_async_remote_copy(
            src_ref=term.at[planes, :, pl.ds(source, 4)],
            dst_ref=term.at[planes, :, pl.ds(target, 4)],
            send_sem=y_send.at[k, way],
            recv_sem=y_recv.at[k, position, way],
            device_id=up if way == 0 else down,
            device_id_type=MESH,
        )

    def x_copy(k, position, way):
        return pltpu.make_async_remote_copy(
            src_ref=packed.at[k, position],
            dst_ref=beside.at[k, way, position],
            send_sem=x_send.at[k, way],
            recv_sem=x_recv.at[k, position, way],
            device_id=right if way == 0 else left,
            device_id_type=MESH,
        )

    def chunk_planes(position):
        return pl.ds(chunk_at(position) * PLANES, PLANES)

    def y_send_start(k, position):
        for way in range(2):
            y_copy(k, chunk_planes(position), position, way).start()

    def x_send_start(k, position):
        for way in range(2):
            x_copy(k, position, way).start()

    def send_edges(k, position):
        y_send_start(k, position)
        x_send_start(k, position)

    lane = lax.broadcasted_iota(jnp.int32, (ROWS, LANES), 1)
    in_left = lax.rem(lane, 8) < 4
    at_edge = (lane < 4) | (lane >= LANES - 4)

    group_of = lane // 8

    def pack(tiles):
        result = jnp.zeros((ROWS, LANES), jnp.float32)
        for g, tile in enumerate(tiles):
            result = jnp.where(group_of == g, pltpu.roll(tile, 8 * g + 4, 1), result)
        return result

    band[...] = band_weights()
    edge[...] = edge_weights()
    for load in loads:
        load.wait()

    @pl.loop(0, CHUNKS)
    def _(position):
        z = chunk_at(position) * PLANES
        packed[0, position] = pack(
            [t0[z + i, o, pl.ds(TOP, ROWS), :] for i in range(PLANES) for o in range(NORB)]
        )

    pl.semaphore_wait(barrier, len(partners) + 3 * oz)

    @pl.loop(0, CHUNKS)
    def _(position):
        send_edges(0, position)

    @pl.when(oz == 1)
    def _():
        signal(ready.at[0], at(0, 0, 1))

    @pl.loop(0, NZ // 4)
    def _(i):
        rows = pl.ds(i * 4, 4)
        pot[rows] = pot[rows] * (1.0 / SPREAD) + (-SHIFT / SPREAD + 3.0 * LAP[0])

    c0, c1, c2, c3 = small[0], small[1], small[2], small[3]

    def inside(k):
        term = terms[k]

        @pl.loop(0, NZ // SPAN)
        def _(span):
            z = span * SPAN
            block = [term[z + i, o, pl.ds(TOP, ROWS), :] for o in range(NORB) for i in range(SPAN)]
            along = MXU_SCALE * jnp.dot(
                split_bf16(jnp.concatenate(block, axis=0)),
                band[...],
                preferred_element_type=jnp.float32,
            )
            for o in range(NORB):
                for half in range(0, ROWS, 8):
                    rows = pl.ds(TOP + half, 8)
                    planes = [
                        term[lax.rem(z + d + NZ, NZ), o, rows, :] for d in range(-4, SPAN + 4)
                    ]
                    for i in range(SPAN):
                        first = (o * SPAN + i) * ROWS + half
                        centre = planes[4 + i]
                        total = pot[z + i, pl.ds(half, 8)] * centre + along[first : first + 8]
                        for j in range(1, 5):
                            total = total + LAP[j] * (planes[4 + i - j] + planes[4 + i + j])
                        if k == 0:
                            t1[z + i, o, rows, :] = total
                        elif k == 1:
                            t2[z + i, o, rows, :] = 2.0 * total - t0[z + i, o, rows, :]
                        else:
                            acc[z + i, o, pl.ds(half, 8)] = (
                                (2.0 * c3) * total
                                + c2 * centre
                                + (c1 - c3) * t1[z + i, o, rows, :]
                                + c0 * t0[z + i, o, rows, :]
                            )

    def side_terms(k, base):
        blocks = []
        for n in range(BATCH):
            for way in range(2):
                x_copy(k, base + n, way).wait_recv()
            blocks.append(
                jnp.where(in_left, beside[k, 0, base + n], beside[k, 1, base + n])
            )
        return MXU_SCALE * jnp.dot(
            split_bf16(jnp.concatenate(blocks, axis=0)),
            edge[...],
            preferred_element_type=jnp.float32,
        )

    def halo_terms(k, position, sides):
        term = terms[k]
        z = chunk_at(position) * PLANES
        totals = []
        for i in range(PLANES):
            for o in range(NORB):
                g = i * NORB + o
                total = jnp.where(at_edge, pltpu.roll(sides, LANES - 4 - 8 * g, 1), 0.0)
                for j in range(1, 5):
                    total = total + LAP[j] * (
                        term[z + i, o, pl.ds(TOP - j, ROWS), :]
                        + term[z + i, o, pl.ds(TOP + j, ROWS), :]
                    )
                totals.append(total)
        return z, totals

    def by_batches(k, finish, send):
        @pl.loop(0, CHUNKS // BATCH)
        def _(batch):
            base = batch * BATCH
            sides = side_terms(k, base)
            for first in range(0, BATCH, GROUP):
                group = range(first, first + GROUP)
                for n in group:
                    for way in range(2):
                        y_copy(k, chunk_planes(base + n), base + n, way).wait_recv()
                for n in group:
                    finish(base + n, *halo_terms(k, base + n, sides[ROWS * n : ROWS * (n + 1)]))
                for n in group:
                    send(base + n, n)

    for k in range(CHEB - 1):
        inside(k)

        def finish(position, z, totals, k=k):
            following = terms[k + 1]
            tiles = []
            for i in range(PLANES):
                for o in range(NORB):
                    total = totals[i * NORB + o]
                    if k > 0:
                        total = 2.0 * total
                    tile = following[z + i, o, pl.ds(TOP, ROWS), :] + total
                    following[z + i, o, pl.ds(TOP, ROWS), :] = tile
                    tiles.append(tile)
            y_send_start(k + 1, position)
            packed[k + 1, position] = pack(tiles)

        def send(position, n, k=k):
            x_send_start(k + 1, position)

        by_batches(k, finish, send)

    def q_copy(position):
        own = position // 4
        straight = jnp.where(position == 2, oz, 0)
        slot = jnp.where(straight == 1, 11, position + 4 * (own + core * (1 - own)))
        to_core = jnp.where(straight == 1, core, 1 - own * (1 - core))
        return pltpu.make_async_remote_copy(
            src_ref=squares.at[position],
            dst_ref=arrived.at[slot],
            send_sem=q_send.at[position],
            recv_sem=q_recv.at[slot],
            device_id=at(distance_at(position), oz - straight, to_core),
            device_id_type=MESH,
        )

    def wait_arrived(slots):
        for slot in slots:
            pltpu.make_async_copy(
                squares.at[0], arrived.at[slot], q_recv.at[slot]
            ).wait()

    def to_owner(on_core):
        return pltpu.make_async_remote_copy(
            src_ref=forward.at[on_core],
            dst_ref=other,
            send_sem=z_send.at[on_core],
            recv_sem=z_recv.at[0],
            device_id=at(0, 1 - oz, on_core),
            device_id_type=MESH,
        )

    inside(CHEB - 1)

    def finish(position, z, totals):
        for i in range(PLANES):
            total = None
            for o in range(NORB):
                value = acc[z + i, o] + (2.0 * c3) * totals[i * NORB + o]
                total = value * value if total is None else total + value * value
            squares[position, i] = total

    def send(position, n):
        if n % 4 != 3:

            @pl.when(position < 4)
            def _():
                q_copy(position).start()

        else:

            @pl.when((position == 3) & (core == 0))
            def _():
                q_copy(position).start()

    by_batches(CHEB - 1, finish, send)

    @pl.when(core == 1)
    def _():
        wait_arrived((4, 5))
        forward[1] = (squares[3] + arrived[4]) + arrived[5]

        @pl.when(oz == 0)
        def _():
            pl.semaphore_wait(ready.at[0], 2)
            wait_arrived((6,))
            forward[1] = forward[1] + arrived[6]

        to_owner(1).start()
        wait_arrived((0, 1, 3))
        forward[0] = (arrived[0] + arrived[1]) + arrived[3]

        @pl.when(oz == 0)
        def _():
            wait_arrived((2,))
            forward[0] = forward[0] + arrived[2]

        to_owner(0).start()

    for position in range(3):
        q_copy(position).wait_send()
    for position in range(4, 7):
        q_copy(position).start()

    for k in range(CHEB):
        for way in range(2):
            pltpu.make_async_remote_copy(
                src_ref=packed.at[k],
                dst_ref=beside.at[k, way],
                send_sem=x_send.at[k, way],
                recv_sem=x_recv.at[k, 0, way],
                device_id=right if way == 0 else left,
                device_id_type=MESH,
            ).wait_send()
            y_copy(k, pl.ds(0, NZ), 0, way).wait_send()
    for position in range(4, 7):
        q_copy(position).wait_send()

    @pl.when(core == 0)
    def _():
        q_copy(3).wait_send()

    wait_arrived((8, 9, 10))
    mine = (squares[7] + arrived[8]) + (arrived[9] + arrived[10])

    @pl.when(core == 1)
    def _():
        for on_core in range(2):
            to_owner(on_core).wait_send()

    to_owner(0).wait_recv()
    out[...] = (mine + other[...]) * (1.0 / 16.0)

    @pl.when(oz == 0)
    def _():
        wait_arrived((11,))
        out[...] = out[...] + arrived[11] * (1.0 / 16.0)


def local(orbitals, potential, coeffs):
    return pl.pallas_call(
        kernel,
        out_shape=jax.ShapeDtypeStruct((PLANES, ROWS, LANES), jnp.float32),
        in_specs=[
            pl.BlockSpec(memory_space=pl.ANY),
            pl.BlockSpec(memory_space=pl.ANY),
            pl.BlockSpec(memory_space=pl.ANY),
        ],
        out_specs=pl.BlockSpec(memory_space=pltpu.VMEM),
        scratch_shapes=[
            pltpu.VMEM((NZ, NORB, 32, LANES), jnp.float32),
            pltpu.VMEM((NZ, NORB, 32, LANES), jnp.float32),
            pltpu.VMEM((NZ, NORB, 32, LANES), jnp.float32),
            pltpu.VMEM((NZ, NORB, ROWS, LANES), jnp.float32),
            pltpu.VMEM((NZ, ROWS, LANES), jnp.float32),
            pltpu.VMEM((2 * LANES, LANES), jnp.bfloat16),
            pltpu.VMEM((2 * LANES, LANES), jnp.bfloat16),
            pltpu.VMEM((CHEB, CHUNKS, ROWS, LANES), jnp.float32),
            pltpu.VMEM((CHEB, 2, CHUNKS, ROWS, LANES), jnp.float32),
            pltpu.VMEM((CHUNKS, PLANES, ROWS, LANES), jnp.float32),
            pltpu.VMEM((12, PLANES, ROWS, LANES), jnp.float32),
            pltpu.VMEM((2, PLANES, ROWS, LANES), jnp.float32),
            pltpu.VMEM((PLANES, ROWS, LANES), jnp.float32),
            pltpu.SMEM((4,), jnp.float32),
            pltpu.SemaphoreType.DMA((NORB + 2,)),
            pltpu.SemaphoreType.DMA((CHEB, 2)),
            pltpu.SemaphoreType.DMA((CHEB, CHUNKS, 2)),
            pltpu.SemaphoreType.DMA((CHEB, 2)),
            pltpu.SemaphoreType.DMA((CHEB, CHUNKS, 2)),
            pltpu.SemaphoreType.DMA((CHUNKS,)),
            pltpu.SemaphoreType.DMA((12,)),
            pltpu.SemaphoreType.DMA((2,)),
            pltpu.SemaphoreType.DMA((1,)),
            pltpu.SemaphoreType.REGULAR((1,)),
        ],
        compiler_params=pltpu.CompilerParams(
            collective_id=0, has_side_effects=True, vmem_limit_bytes=55000 * 2**10
        ),
        name="chebyshev",
    )(orbitals, potential, coeffs)


def solution(mesh):
    in_specs = (P("orb", None, "gy", "gx"), P(None, "gy", "gx"), P())
    out_specs = P("orb", "gy", "gx")
    return jax.shard_map(local, mesh=mesh, in_specs=in_specs, out_specs=out_specs, check_vma=False)
```

```python
import jax
import jax.numpy as jnp
from jax import lax
from jax.experimental import pallas as pl
from jax.experimental.pallas import tpu as pltpu
from jax.sharding import PartitionSpec as P

MESH = pl.DeviceIdType.MESH

CHEB = 3
STENCIL = (-205.0 / 72.0, 8.0 / 5.0, -1.0 / 5.0, 8.0 / 315.0, -1.0 / 560.0)
WHOLE = (0.0, 8064.0, -1008.0, 128.0, -9.0)
SHIFT = 5.875
SPREAD = 6.0
LAP = tuple(-0.5 * s / SPREAD for s in STENCIL)
MXU_SCALE = -0.5 / SPREAD / 5040.0

NZ = 48
NORB = 2
ROWS = 16
LANES = 128
CHUNKS = 8
PLANES = NZ // CHUNKS
TILES = PLANES * NORB
SPAN = 12
BATCH = 2
GROUP = 1
TOP = 8


def split_bf16(values):
    high = values.astype(jnp.bfloat16)
    low = (values - high.astype(jnp.float32)).astype(jnp.bfloat16)
    return jnp.concatenate([high, low], axis=1)


def band_weights():
    row = lax.rem(lax.broadcasted_iota(jnp.int32, (2 * LANES, LANES), 0), LANES)
    column = lax.broadcasted_iota(jnp.int32, (2 * LANES, LANES), 1)
    distance = jnp.abs(row - column)
    weights = jnp.zeros((2 * LANES, LANES), jnp.float32)
    for j in range(1, 5):
        weights = jnp.where(distance == j, WHOLE[j], weights)
    return weights.astype(jnp.bfloat16)


def edge_weights():
    row = lax.rem(lax.broadcasted_iota(jnp.int32, (2 * LANES, LANES), 0), LANES)
    column = lax.broadcasted_iota(jnp.int32, (2 * LANES, LANES), 1)
    distance = jnp.abs(row - column)
    crosses = (row // 8 == column // 8) & (row // 4 != column // 4)
    weights = jnp.zeros((2 * LANES, LANES), jnp.float32)
    for j in range(1, 5):
        weights = jnp.where(crosses & (distance == j), WHOLE[j], weights)
    return weights.astype(jnp.bfloat16)


def kernel(
    orbitals, potential, coeffs, out,
    t0, t1, t2, acc, pot, band, edge, packed, beside, squares, arrived, forward, other,
    small, local_sem, y_send, y_recv, x_send, x_recv, q_send, q_recv, z_send, z_recv, ready,
):
    terms = (t0, t1, t2)
    orb, gx, gy = lax.axis_index("orb"), lax.axis_index("gx"), lax.axis_index("gy")
    n_gx, n_gy = lax.axis_size("gx"), lax.axis_size("gy")
    ox, oz = orb // 2, lax.rem(orb, 2)

    def distance_at(position):
        step = lax.rem(position, 4)
        return lax.rem(1 + 2 * step - 3 * (step // 2), 4)

    def chunk_at(position):
        to_x = lax.rem(ox + distance_at(position), 4)
        to_z = lax.rem(oz + 1 + position // 4, 2)
        return to_x * 2 + to_z

    up, down = {"gy": lax.rem(gy + 1, n_gy)}, {"gy": lax.rem(gy + n_gy - 1, n_gy)}
    right, left = {"gx": lax.rem(gx + 1, n_gx)}, {"gx": lax.rem(gx + n_gx - 1, n_gx)}

    core = lax.rem(gy, 2)

    def at(distance, z, on_core):
        return {"orb": lax.rem(ox + distance, 4) * 2 + z, "gy": gy - core + on_core}

    barrier = pltpu.get_barrier_semaphore()

    def signal(semaphore, device):
        pl.semaphore_signal(semaphore, inc=1, device_id=device, device_id_type=MESH)

    partners = [up, down, right, left]
    for to_core in (core, 1 - core):
        partners += [at(distance, oz, to_core) for distance in (2, 1, 3)]
    for partner in partners:
        signal(barrier, partner)

    @pl.when(oz == 0)
    def _():
        for to_core in range(2):
            signal(barrier, at(0, 1, to_core))
        signal(barrier, at(2, 1, core))

    loads = [
        pltpu.make_async_copy(
            orbitals.at[o], t0.at[:, o, pl.ds(TOP, ROWS)], local_sem.at[o]
        )
        for o in range(NORB)
    ]
    loads.append(pltpu.make_async_copy(potential, pot, local_sem.at[NORB]))
    loads.append(pltpu.make_async_copy(coeffs, small, local_sem.at[NORB + 1]))
    for load in loads:
        load.start()

    def y_copy(k, planes, position, way):
        term = terms[k]
        source, target = (TOP + ROWS - 4, TOP - 4) if way == 0 else (TOP, TOP + ROWS)
        return pltpu.make_async_remote_copy(
            src_ref=term.at[planes, :, pl.ds(source, 4)],
            dst_ref=term.at[planes, :, pl.ds(target, 4)],
            send_sem=y_send.at[k, way],
            recv_sem=y_recv.at[k, position, way],
            device_id=up if way == 0 else down,
            device_id_type=MESH,
        )

    def x_copy(k, position, way):
        return pltpu.make_async_remote_copy(
            src_ref=packed.at[k, position],
            dst_ref=beside.at[k, way, position],
            send_sem=x_send.at[k, way],
            recv_sem=x_recv.at[k, position, way],
            device_id=right if way == 0 else left,
            device_id_type=MESH,
        )

    def chunk_planes(position):
        return pl.ds(chunk_at(position) * PLANES, PLANES)

    def y_send_start(k, position):
        for way in range(2):
            y_copy(k, chunk_planes(position), position, way).start()

    def x_send_start(k, position):
        for way in range(2):
            x_copy(k, position, way).start()

    def send_edges(k, position):
        y_send_start(k, position)
        x_send_start(k, position)

    lane = lax.broadcasted_iota(jnp.int32, (ROWS, LANES), 1)
    in_left = lax.rem(lane, 8) < 4
    at_edge = (lane < 4) | (lane >= LANES - 4)

    group_of = lane // 8

    def pack(tiles):
        result = jnp.zeros((ROWS, LANES), jnp.float32)
        for g, tile in enumerate(tiles):
            result = jnp.where(group_of == g, pltpu.roll(tile, 8 * g + 4, 1), result)
        return result

    band[...] = band_weights()
    edge[...] = edge_weights()
    for load in loads:
        load.wait()

    @pl.loop(0, CHUNKS)
    def _(position):
        z = chunk_at(position) * PLANES
        packed[0, position] = pack(
            [t0[z + i, o, pl.ds(TOP, ROWS), :] for i in range(PLANES) for o in range(NORB)]
        )

    pl.semaphore_wait(barrier, len(partners) + 3 * oz)

    @pl.loop(0, CHUNKS)
    def _(position):
        send_edges(0, position)

    @pl.when(oz == 1)
    def _():
        signal(ready.at[0], at(0, 0, 1))

    @pl.loop(0, NZ // 4)
    def _(i):
        rows = pl.ds(i * 4, 4)
        pot[rows] = pot[rows] * (1.0 / SPREAD) + (-SHIFT / SPREAD + 3.0 * LAP[0])

    c0, c1, c2, c3 = small[0], small[1], small[2], small[3]

    def inside(k):
        term = terms[k]

        @pl.loop(0, NZ // SPAN)
        def _(span):
            z = span * SPAN
            block = [term[z + i, o, pl.ds(TOP, ROWS), :] for o in range(NORB) for i in range(SPAN)]
            along = MXU_SCALE * jnp.dot(
                split_bf16(jnp.concatenate(block, axis=0)),
                band[...],
                preferred_element_type=jnp.float32,
            )
            for o in range(NORB):
                for half in range(0, ROWS, 8):
                    rows = pl.ds(TOP + half, 8)
                    planes = [
                        term[lax.rem(z + d + NZ, NZ), o, rows, :] for d in range(-4, SPAN + 4)
                    ]
                    for i in range(SPAN):
                        first = (o * SPAN + i) * ROWS + half
                        centre = planes[4 + i]
                        total = pot[z + i, pl.ds(half, 8)] * centre + along[first : first + 8]
                        for j in range(1, 5):
                            total = total + LAP[j] * (planes[4 + i - j] + planes[4 + i + j])
                        if k == 0:
                            t1[z + i, o, rows, :] = total
                        elif k == 1:
                            t2[z + i, o, rows, :] = 2.0 * total - t0[z + i, o, rows, :]
                        else:
                            acc[z + i, o, pl.ds(half, 8)] = (
                                (2.0 * c3) * total
                                + c2 * centre
                                + (c1 - c3) * t1[z + i, o, rows, :]
                                + c0 * t0[z + i, o, rows, :]
                            )

    def side_terms(k, base):
        blocks = []
        for n in range(BATCH):
            for way in range(2):
                x_copy(k, base + n, way).wait_recv()
            blocks.append(
                jnp.where(in_left, beside[k, 0, base + n], beside[k, 1, base + n])
            )
        return MXU_SCALE * jnp.dot(
            split_bf16(jnp.concatenate(blocks, axis=0)),
            edge[...],
            preferred_element_type=jnp.float32,
        )

    def halo_terms(k, position, sides):
        term = terms[k]
        z = chunk_at(position) * PLANES
        totals = []
        for i in range(PLANES):
            for o in range(NORB):
                g = i * NORB + o
                total = jnp.where(at_edge, pltpu.roll(sides, LANES - 4 - 8 * g, 1), 0.0)
                for j in range(1, 5):
                    total = total + LAP[j] * (
                        term[z + i, o, pl.ds(TOP - j, ROWS), :]
                        + term[z + i, o, pl.ds(TOP + j, ROWS), :]
                    )
                totals.append(total)
        return z, totals

    def by_batches(k, finish, send):
        @pl.loop(0, CHUNKS // BATCH)
        def _(batch):
            base = batch * BATCH
            sides = side_terms(k, base)
            for first in range(0, BATCH, GROUP):
                group = range(first, first + GROUP)
                for n in group:
                    for way in range(2):
                        y_copy(k, chunk_planes(base + n), base + n, way).wait_recv()
                for n in group:
                    finish(base + n, *halo_terms(k, base + n, sides[ROWS * n : ROWS * (n + 1)]))
                for n in group:
                    send(base + n, n)

    for k in range(CHEB - 1):
        inside(k)

        def finish(position, z, totals, k=k):
            following = terms[k + 1]
            tiles = []
            for i in range(PLANES):
                for o in range(NORB):
                    total = totals[i * NORB + o]
                    if k > 0:
                        total = 2.0 * total
                    tile = following[z + i, o, pl.ds(TOP, ROWS), :] + total
                    following[z + i, o, pl.ds(TOP, ROWS), :] = tile
                    tiles.append(tile)
            y_send_start(k + 1, position)
            packed[k + 1, position] = pack(tiles)

        def send(position, n, k=k):
            x_send_start(k + 1, position)

        by_batches(k, finish, send)

    def q_copy(position):
        own = position // 4
        straight = jnp.where(position == 2, oz, 0)
        slot = jnp.where(straight == 1, 11, position + 4 * (own + core * (1 - own)))
        to_core = jnp.where(straight == 1, core, 1 - own * (1 - core))
        return pltpu.make_async_remote_copy(
            src_ref=squares.at[position],
            dst_ref=arrived.at[slot],
            send_sem=q_send.at[position],
            recv_sem=q_recv.at[slot],
            device_id=at(distance_at(position), oz - straight, to_core),
            device_id_type=MESH,
        )

    def wait_arrived(slots):
        for slot in slots:
            pltpu.make_async_copy(
                squares.at[0], arrived.at[slot], q_recv.at[slot]
            ).wait()

    def to_owner(on_core):
        return pltpu.make_async_remote_copy(
            src_ref=forward.at[on_core],
            dst_ref=other,
            send_sem=z_send.at[on_core],
            recv_sem=z_recv.at[0],
            device_id=at(0, 1 - oz, on_core),
            device_id_type=MESH,
        )

    inside(CHEB - 1)

    def finish(position, z, totals):
        for i in range(PLANES):
            total = None
            for o in range(NORB):
                value = acc[z + i, o] + (2.0 * c3) * totals[i * NORB + o]
                total = value * value if total is None else total + value * value
            squares[position, i] = total

    def send(position, n):
        @pl.when((position < 3) | ((position == 3) & (core == 0)))
        def _():
            q_copy(position).start()

    by_batches(CHEB - 1, finish, send)

    @pl.when(core == 1)
    def _():
        wait_arrived((4, 5))
        forward[1] = (squares[3] + arrived[4]) + arrived[5]

        @pl.when(oz == 0)
        def _():
            pl.semaphore_wait(ready.at[0], 2)
            wait_arrived((6,))
            forward[1] = forward[1] + arrived[6]

        to_owner(1).start()
        wait_arrived((0, 1, 3))
        forward[0] = (arrived[0] + arrived[1]) + arrived[3]

        @pl.when(oz == 0)
        def _():
            wait_arrived((2,))
            forward[0] = forward[0] + arrived[2]

        to_owner(0).start()

    for position in range(3):
        q_copy(position).wait_send()
    for position in range(4, 7):
        q_copy(position).start()

    for k in range(CHEB):
        for way in range(2):
            pltpu.make_async_remote_copy(
                src_ref=packed.at[k],
                dst_ref=beside.at[k, way],
                send_sem=x_send.at[k, way],
                recv_sem=x_recv.at[k, 0, way],
                device_id=right if way == 0 else left,
                device_id_type=MESH,
            ).wait_send()
            y_copy(k, pl.ds(0, NZ), 0, way).wait_send()
    for position in range(4, 7):
        q_copy(position).wait_send()

    @pl.when(core == 0)
    def _():
        q_copy(3).wait_send()

    wait_arrived((8, 9, 10))
    mine = (squares[7] + arrived[8]) + (arrived[9] + arrived[10])

    @pl.when(core == 1)
    def _():
        for on_core in range(2):
            to_owner(on_core).wait_send()

    to_owner(0).wait_recv()
    out[...] = (mine + other[...]) * (1.0 / 16.0)

    @pl.when(oz == 0)
    def _():
        wait_arrived((11,))
        out[...] = out[...] + arrived[11] * (1.0 / 16.0)


def local(orbitals, potential, coeffs):
    return pl.pallas_call(
        kernel,
        out_shape=jax.ShapeDtypeStruct((PLANES, ROWS, LANES), jnp.float32),
        in_specs=[
            pl.BlockSpec(memory_space=pl.ANY),
            pl.BlockSpec(memory_space=pl.ANY),
            pl.BlockSpec(memory_space=pl.ANY),
        ],
        out_specs=pl.BlockSpec(memory_space=pltpu.VMEM),
        scratch_shapes=[
            pltpu.VMEM((NZ, NORB, 32, LANES), jnp.float32),
            pltpu.VMEM((NZ, NORB, 32, LANES), jnp.float32),
            pltpu.VMEM((NZ, NORB, 32, LANES), jnp.float32),
            pltpu.VMEM((NZ, NORB, ROWS, LANES), jnp.float32),
            pltpu.VMEM((NZ, ROWS, LANES), jnp.float32),
            pltpu.VMEM((2 * LANES, LANES), jnp.bfloat16),
            pltpu.VMEM((2 * LANES, LANES), jnp.bfloat16),
            pltpu.VMEM((CHEB, CHUNKS, ROWS, LANES), jnp.float32),
            pltpu.VMEM((CHEB, 2, CHUNKS, ROWS, LANES), jnp.float32),
            pltpu.VMEM((CHUNKS, PLANES, ROWS, LANES), jnp.float32),
            pltpu.VMEM((12, PLANES, ROWS, LANES), jnp.float32),
            pltpu.VMEM((2, PLANES, ROWS, LANES), jnp.float32),
            pltpu.VMEM((PLANES, ROWS, LANES), jnp.float32),
            pltpu.SMEM((4,), jnp.float32),
            pltpu.SemaphoreType.DMA((NORB + 2,)),
            pltpu.SemaphoreType.DMA((CHEB, 2)),
            pltpu.SemaphoreType.DMA((CHEB, CHUNKS, 2)),
            pltpu.SemaphoreType.DMA((CHEB, 2)),
            pltpu.SemaphoreType.DMA((CHEB, CHUNKS, 2)),
            pltpu.SemaphoreType.DMA((CHUNKS,)),
            pltpu.SemaphoreType.DMA((12,)),
            pltpu.SemaphoreType.DMA((2,)),
            pltpu.SemaphoreType.DMA((1,)),
            pltpu.SemaphoreType.REGULAR((1,)),
        ],
        compiler_params=pltpu.CompilerParams(
            collective_id=0, has_side_effects=True, vmem_limit_bytes=55000 * 2**10
        ),
        name="chebyshev",
    )(orbitals, potential, coeffs)


def solution(mesh):
    in_specs = (P("orb", None, "gy", "gx"), P(None, "gy", "gx"), P())
    out_specs = P("orb", "gy", "gx")
    return jax.shard_map(local, mesh=mesh, in_specs=in_specs, out_specs=out_specs, check_vma=False)
```

```python
import jax
import jax.numpy as jnp
from jax import lax
from jax.experimental import pallas as pl
from jax.experimental.pallas import tpu as pltpu
from jax.sharding import PartitionSpec as P

MESH = pl.DeviceIdType.MESH

CHEB = 3
STENCIL = (-205.0 / 72.0, 8.0 / 5.0, -1.0 / 5.0, 8.0 / 315.0, -1.0 / 560.0)
WHOLE = (0.0, 8064.0, -1008.0, 128.0, -9.0)
SHIFT = 5.875
SPREAD = 6.0
LAP = tuple(-0.5 * s / SPREAD for s in STENCIL)
MXU_SCALE = -0.5 / SPREAD / 5040.0

NZ = 48
NORB = 2
ROWS = 16
LANES = 128
CHUNKS = 8
PLANES = NZ // CHUNKS
TILES = PLANES * NORB
SPAN = 12
BATCH = 2
GROUP = 1
TOP = 8


def split_bf16(values):
    high = values.astype(jnp.bfloat16)
    low = (values - high.astype(jnp.float32)).astype(jnp.bfloat16)
    return jnp.concatenate([high, low], axis=1)


def band_weights():
    row = lax.rem(lax.broadcasted_iota(jnp.int32, (2 * LANES, LANES), 0), LANES)
    column = lax.broadcasted_iota(jnp.int32, (2 * LANES, LANES), 1)
    distance = jnp.abs(row - column)
    weights = jnp.zeros((2 * LANES, LANES), jnp.float32)
    for j in range(1, 5):
        weights = jnp.where(distance == j, WHOLE[j], weights)
    return weights.astype(jnp.bfloat16)


def edge_weights():
    row = lax.rem(lax.broadcasted_iota(jnp.int32, (2 * LANES, LANES), 0), LANES)
    column = lax.broadcasted_iota(jnp.int32, (2 * LANES, LANES), 1)
    distance = jnp.abs(row - column)
    crosses = (row // 8 == column // 8) & (row // 4 != column // 4)
    weights = jnp.zeros((2 * LANES, LANES), jnp.float32)
    for j in range(1, 5):
        weights = jnp.where(crosses & (distance == j), WHOLE[j], weights)
    return weights.astype(jnp.bfloat16)


def kernel(
    orbitals, potential, coeffs, out,
    t0, t1, t2, acc, pot, band, edge, packed, beside, squares, arrived, forward, other,
    small, local_sem, y_send, y_recv, x_send, x_recv, q_send, q_recv, z_send, z_recv, ready,
):
    terms = (t0, t1, t2)
    orb, gx, gy = lax.axis_index("orb"), lax.axis_index("gx"), lax.axis_index("gy")
    n_gx, n_gy = lax.axis_size("gx"), lax.axis_size("gy")
    ox, oz = orb // 2, lax.rem(orb, 2)

    def distance_at(position):
        step = lax.rem(position, 4)
        return lax.rem(1 + 2 * step - 3 * (step // 2), 4)

    def chunk_at(position):
        to_x = lax.rem(ox + distance_at(position), 4)
        to_z = lax.rem(oz + 1 + position // 4, 2)
        return to_x * 2 + to_z

    up, down = {"gy": lax.rem(gy + 1, n_gy)}, {"gy": lax.rem(gy + n_gy - 1, n_gy)}
    right, left = {"gx": lax.rem(gx + 1, n_gx)}, {"gx": lax.rem(gx + n_gx - 1, n_gx)}

    core = lax.rem(gy, 2)

    def at(distance, z, on_core):
        return {"orb": lax.rem(ox + distance, 4) * 2 + z, "gy": gy - core + on_core}

    barrier = pltpu.get_barrier_semaphore()

    def signal(semaphore, device):
        pl.semaphore_signal(semaphore, inc=1, device_id=device, device_id_type=MESH)

    partners = [up, down, right, left]
    for to_core in (core, 1 - core):
        partners += [at(distance, oz, to_core) for distance in (2, 1, 3)]
    for partner in partners:
        signal(barrier, partner)

    @pl.when(oz == 0)
    def _():
        for to_core in range(2):
            signal(barrier, at(0, 1, to_core))
        signal(barrier, at(2, 1, core))

    loads = [
        pltpu.make_async_copy(
            orbitals.at[o], t0.at[:, o, pl.ds(TOP, ROWS)], local_sem.at[o]
        )
        for o in range(NORB)
    ]
    loads.append(pltpu.make_async_copy(potential, pot, local_sem.at[NORB]))
    loads.append(pltpu.make_async_copy(coeffs, small, local_sem.at[NORB + 1]))
    for load in loads:
        load.start()

    def y_copy(k, planes, position, way):
        term = terms[k]
        source, target = (TOP + ROWS - 4, TOP - 4) if way == 0 else (TOP, TOP + ROWS)
        return pltpu.make_async_remote_copy(
            src_ref=term.at[planes, :, pl.ds(source, 4)],
            dst_ref=term.at[planes, :, pl.ds(target, 4)],
            send_sem=y_send.at[k, way],
            recv_sem=y_recv.at[k, position, way],
            device_id=up if way == 0 else down,
            device_id_type=MESH,
        )

    def x_copy(k, position, way):
        return pltpu.make_async_remote_copy(
            src_ref=packed.at[k, position],
            dst_ref=beside.at[k, way, position],
            send_sem=x_send.at[k, way],
            recv_sem=x_recv.at[k, position, way],
            device_id=right if way == 0 else left,
            device_id_type=MESH,
        )

    def chunk_planes(position):
        return pl.ds(chunk_at(position) * PLANES, PLANES)

    def y_send_start(k, position):
        for way in range(2):
            y_copy(k, chunk_planes(position), position, way).start()

    def x_send_start(k, position):
        for way in range(2):
            x_copy(k, position, way).start()

    def send_edges(k, position):
        y_send_start(k, position)
        x_send_start(k, position)

    lane = lax.broadcasted_iota(jnp.int32, (ROWS, LANES), 1)
    in_left = lax.rem(lane, 8) < 4
    at_edge = (lane < 4) | (lane >= LANES - 4)

    group_of = lane // 8

    def pack(tiles):
        result = jnp.zeros((ROWS, LANES), jnp.float32)
        for g, tile in enumerate(tiles):
            result = jnp.where(group_of == g, pltpu.roll(tile, 8 * g + 4, 1), result)
        return result

    band[...] = band_weights()
    edge[...] = edge_weights()
    for load in loads:
        load.wait()

    @pl.loop(0, CHUNKS)
    def _(position):
        z = chunk_at(position) * PLANES
        packed[0, position] = pack(
            [t0[z + i, o, pl.ds(TOP, ROWS), :] for i in range(PLANES) for o in range(NORB)]
        )

    pl.semaphore_wait(barrier, len(partners) + 3 * oz)

    @pl.loop(0, CHUNKS)
    def _(position):
        send_edges(0, position)

    @pl.when(oz == 1)
    def _():
        signal(ready.at[0], at(0, 0, 1))

    @pl.loop(0, NZ // 4)
    def _(i):
        rows = pl.ds(i * 4, 4)
        pot[rows] = pot[rows] * (1.0 / SPREAD) + (-SHIFT / SPREAD + 3.0 * LAP[0])

    c0, c1, c2, c3 = small[0], small[1], small[2], small[3]

    def inside(k):
        term = terms[k]

        @pl.loop(0, NZ // SPAN)
        def _(span):
            z = span * SPAN
            block = [term[z + i, o, pl.ds(TOP, ROWS), :] for o in range(NORB) for i in range(SPAN)]
            along = MXU_SCALE * jnp.dot(
                split_bf16(jnp.concatenate(block, axis=0)),
                band[...],
                preferred_element_type=jnp.float32,
            )
            for o in range(NORB):
                for half in range(0, ROWS, 8):
                    rows = pl.ds(TOP + half, 8)
                    planes = [
                        term[lax.rem(z + d + NZ, NZ), o, rows, :] for d in range(-4, SPAN + 4)
                    ]
                    for i in range(SPAN):
                        first = (o * SPAN + i) * ROWS + half
                        centre = planes[4 + i]
                        total = pot[z + i, pl.ds(half, 8)] * centre + along[first : first + 8]
                        for j in range(1, 5):
                            total = total + LAP[j] * (planes[4 + i - j] + planes[4 + i + j])
                        if k == 0:
                            t1[z + i, o, rows, :] = total
                        elif k == 1:
                            t2[z + i, o, rows, :] = 2.0 * total - t0[z + i, o, rows, :]
                        else:
                            acc[z + i, o, pl.ds(half, 8)] = (
                                (2.0 * c3) * total
                                + c2 * centre
                                + (c1 - c3) * t1[z + i, o, rows, :]
                                + c0 * t0[z + i, o, rows, :]
                            )

    def side_terms(k, base):
        blocks = []
        for n in range(BATCH):
            for way in range(2):
                x_copy(k, base + n, way).wait_recv()
            blocks.append(
                jnp.where(in_left, beside[k, 0, base + n], beside[k, 1, base + n])
            )
        return MXU_SCALE * jnp.dot(
            split_bf16(jnp.concatenate(blocks, axis=0)),
            edge[...],
            preferred_element_type=jnp.float32,
        )

    def halo_terms(k, position, sides):
        term = terms[k]
        z = chunk_at(position) * PLANES
        totals = []
        for i in range(PLANES):
            for o in range(NORB):
                g = i * NORB + o
                total = jnp.where(at_edge, pltpu.roll(sides, LANES - 4 - 8 * g, 1), 0.0)
                for j in range(1, 5):
                    total = total + LAP[j] * (
                        term[z + i, o, pl.ds(TOP - j, ROWS), :]
                        + term[z + i, o, pl.ds(TOP + j, ROWS), :]
                    )
                totals.append(total)
        return z, totals

    def by_batches(k, finish, send):
        @pl.loop(0, CHUNKS // BATCH)
        def _(batch):
            base = batch * BATCH
            sides = side_terms(k, base)
            for first in range(0, BATCH, GROUP):
                group = range(first, first + GROUP)
                for n in group:
                    for way in range(2):
                        y_copy(k, chunk_planes(base + n), base + n, way).wait_recv()
                for n in group:
                    finish(base + n, *halo_terms(k, base + n, sides[ROWS * n : ROWS * (n + 1)]))
                for n in group:
                    send(base + n, n)

    for k in range(CHEB - 1):
        inside(k)

        def finish(position, z, totals, k=k):
            following = terms[k + 1]
            tiles = []
            for i in range(PLANES):
                for o in range(NORB):
                    total = totals[i * NORB + o]
                    if k > 0:
                        total = 2.0 * total
                    tile = following[z + i, o, pl.ds(TOP, ROWS), :] + total
                    following[z + i, o, pl.ds(TOP, ROWS), :] = tile
                    tiles.append(tile)
            y_send_start(k + 1, position)
            packed[k + 1, position] = pack(tiles)

        def send(position, n, k=k):
            x_send_start(k + 1, position)

        by_batches(k, finish, send)

    def q_copy(position):
        own = position // 4
        straight = jnp.where(position == 2, oz, 0)
        slot = jnp.where(straight == 1, 11, position + 4 * (own + core * (1 - own)))
        to_core = jnp.where(straight == 1, core, 1 - own * (1 - core))
        return pltpu.make_async_remote_copy(
            src_ref=squares.at[position],
            dst_ref=arrived.at[slot],
            send_sem=q_send.at[position],
            recv_sem=q_recv.at[slot],
            device_id=at(distance_at(position), oz - straight, to_core),
            device_id_type=MESH,
        )

    def wait_arrived(slots):
        for slot in slots:
            pltpu.make_async_copy(
                squares.at[0], arrived.at[slot], q_recv.at[slot]
            ).wait()

    def to_owner(on_core):
        return pltpu.make_async_remote_copy(
            src_ref=forward.at[on_core],
            dst_ref=other,
            send_sem=z_send.at[on_core],
            recv_sem=z_recv.at[0],
            device_id=at(0, 1 - oz, on_core),
            device_id_type=MESH,
        )

    inside(CHEB - 1)

    def finish(position, z, totals):
        for i in range(PLANES):
            total = None
            for o in range(NORB):
                value = acc[z + i, o] + (2.0 * c3) * totals[i * NORB + o]
                total = value * value if total is None else total + value * value
            squares[position, i] = total

    def send(position, n):
        @pl.when((position < 3) | ((position == 3) & (core == 0)))
        def _():
            q_copy(position).start()

    by_batches(CHEB - 1, finish, send)

    @pl.when(core == 1)
    def _():
        wait_arrived((4, 5))
        forward[1] = (squares[3] + arrived[4]) + arrived[5]

        @pl.when(oz == 0)
        def _():
            pl.semaphore_wait(ready.at[0], 2)
            wait_arrived((6,))
            forward[1] = forward[1] + arrived[6]

        to_owner(1).start()
        wait_arrived((0, 1, 3))
        forward[0] = (arrived[0] + arrived[1]) + arrived[3]

        @pl.when(oz == 0)
        def _():
            wait_arrived((2,))
            forward[0] = forward[0] + arrived[2]

        to_owner(0).start()

    for position in range(3):
        q_copy(position).wait_send()
    for position in range(4, 7):
        q_copy(position).start()

    for k in range(CHEB):
        for way in range(2):
            pltpu.make_async_remote_copy(
                src_ref=packed.at[k],
                dst_ref=beside.at[k, way],
                send_sem=x_send.at[k, way],
                recv_sem=x_recv.at[k, 0, way],
                device_id=right if way == 0 else left,
                device_id_type=MESH,
            ).wait_send()
            y_copy(k, pl.ds(0, NZ), 0, way).wait_send()
    for position in range(4, 7):
        q_copy(position).wait_send()

    @pl.when(core == 0)
    def _():
        q_copy(3).wait_send()

    wait_arrived((8, 9, 10))
    mine = (squares[7] + arrived[8]) + (arrived[9] + arrived[10])

    @pl.when(core == 1)
    def _():
        for on_core in range(2):
            to_owner(on_core).wait_send()

    to_owner(0).wait_recv()
    out[...] = (mine + other[...]) * (1.0 / 16.0)

    @pl.when(oz == 0)
    def _():
        wait_arrived((11,))
        out[...] = out[...] + arrived[11] * (1.0 / 16.0)


def local(orbitals, potential, coeffs):
    return pl.pallas_call(
        kernel,
        out_shape=jax.ShapeDtypeStruct((PLANES, ROWS, LANES), jnp.float32),
        in_specs=[
            pl.BlockSpec(memory_space=pl.ANY),
            pl.BlockSpec(memory_space=pl.ANY),
            pl.BlockSpec(memory_space=pl.ANY),
        ],
        out_specs=pl.BlockSpec(memory_space=pltpu.VMEM),
        scratch_shapes=[
            pltpu.VMEM((NZ, NORB, 32, LANES), jnp.float32),
            pltpu.VMEM((NZ, NORB, 32, LANES), jnp.float32),
            pltpu.VMEM((NZ, NORB, 32, LANES), jnp.float32),
            pltpu.VMEM((NZ, NORB, ROWS, LANES), jnp.float32),
            pltpu.VMEM((NZ, ROWS, LANES), jnp.float32),
            pltpu.VMEM((2 * LANES, LANES), jnp.bfloat16),
            pltpu.VMEM((2 * LANES, LANES), jnp.bfloat16),
            pltpu.VMEM((CHEB, CHUNKS, ROWS, LANES), jnp.float32),
            pltpu.VMEM((CHEB, 2, CHUNKS, ROWS, LANES), jnp.float32),
            pltpu.VMEM((CHUNKS, PLANES, ROWS, LANES), jnp.float32),
            pltpu.VMEM((12, PLANES, ROWS, LANES), jnp.float32),
            pltpu.VMEM((2, PLANES, ROWS, LANES), jnp.float32),
            pltpu.VMEM((PLANES, ROWS, LANES), jnp.float32),
            pltpu.SMEM((4,), jnp.float32),
            pltpu.SemaphoreType.DMA((NORB + 2,)),
            pltpu.SemaphoreType.DMA((CHEB, 2)),
            pltpu.SemaphoreType.DMA((CHEB, CHUNKS, 2)),
            pltpu.SemaphoreType.DMA((CHEB, 2)),
            pltpu.SemaphoreType.DMA((CHEB, CHUNKS, 2)),
            pltpu.SemaphoreType.DMA((CHUNKS,)),
            pltpu.SemaphoreType.DMA((12,)),
            pltpu.SemaphoreType.DMA((2,)),
            pltpu.SemaphoreType.DMA((1,)),
            pltpu.SemaphoreType.REGULAR((1,)),
        ],
        compiler_params=pltpu.CompilerParams(
            collective_id=0, has_side_effects=True, vmem_limit_bytes=48000 * 2**10
        ),
        name="chebyshev",
    )(*(pltpu.with_memory_space_constraint(a, pltpu.HBM) for a in (orbitals, potential, coeffs)))


def solution(mesh):
    in_specs = (P("orb", None, "gy", "gx"), P(None, "gy", "gx"), P())
    out_specs = P("orb", "gy", "gx")
    return jax.shard_map(local, mesh=mesh, in_specs=in_specs, out_specs=out_specs, check_vma=False)
```

```python
import jax
import jax.numpy as jnp
from jax import lax
from jax.experimental import pallas as pl
from jax.experimental.pallas import tpu as pltpu
from jax.sharding import PartitionSpec as P

MESH = pl.DeviceIdType.MESH

CHEB = 3
STENCIL = (-205.0 / 72.0, 8.0 / 5.0, -1.0 / 5.0, 8.0 / 315.0, -1.0 / 560.0)
WHOLE = (0.0, 8064.0, -1008.0, 128.0, -9.0)
SHIFT = 5.875
SPREAD = 6.0
LAP = tuple(-0.5 * s / SPREAD for s in STENCIL)
MXU_SCALE = -0.5 / SPREAD / 5040.0

NZ = 48
NORB = 2
ROWS = 16
LANES = 128
CHUNKS = 8
PLANES = NZ // CHUNKS
TILES = PLANES * NORB
SPAN = 12
BATCH = 2
GROUP = 1
TOP = 8


def split_bf16(values):
    high = values.astype(jnp.bfloat16)
    low = (values - high.astype(jnp.float32)).astype(jnp.bfloat16)
    return jnp.concatenate([high, low], axis=1)


def band_weights():
    row = lax.rem(lax.broadcasted_iota(jnp.int32, (2 * LANES, LANES), 0), LANES)
    column = lax.broadcasted_iota(jnp.int32, (2 * LANES, LANES), 1)
    distance = jnp.abs(row - column)
    weights = jnp.zeros((2 * LANES, LANES), jnp.float32)
    for j in range(1, 5):
        weights = jnp.where(distance == j, WHOLE[j], weights)
    return weights.astype(jnp.bfloat16)


def edge_weights():
    row = lax.rem(lax.broadcasted_iota(jnp.int32, (2 * LANES, LANES), 0), LANES)
    column = lax.broadcasted_iota(jnp.int32, (2 * LANES, LANES), 1)
    distance = jnp.abs(row - column)
    crosses = (row // 8 == column // 8) & (row // 4 != column // 4)
    weights = jnp.zeros((2 * LANES, LANES), jnp.float32)
    for j in range(1, 5):
        weights = jnp.where(crosses & (distance == j), WHOLE[j], weights)
    return weights.astype(jnp.bfloat16)


def kernel(
    orbitals, potential, coeffs, out,
    t0, t1, t2, acc, pot, band, edge, packed, beside, squares, arrived, forward, other,
    small, local_sem, y_send, y_recv, x_send, x_recv, q_send, q_recv, z_send, z_recv, ready,
):
    terms = (t0, t1, t2)
    orb, gx, gy = lax.axis_index("orb"), lax.axis_index("gx"), lax.axis_index("gy")
    n_gx, n_gy = lax.axis_size("gx"), lax.axis_size("gy")
    ox, oz = orb // 2, lax.rem(orb, 2)

    def distance_at(position):
        step = lax.rem(position, 4)
        return lax.rem(1 + 2 * step - 3 * (step // 2), 4)

    def chunk_at(position):
        to_x = lax.rem(ox + distance_at(position), 4)
        to_z = lax.rem(oz + 1 + position // 4, 2)
        return to_x * 2 + to_z

    up, down = {"gy": lax.rem(gy + 1, n_gy)}, {"gy": lax.rem(gy + n_gy - 1, n_gy)}
    right, left = {"gx": lax.rem(gx + 1, n_gx)}, {"gx": lax.rem(gx + n_gx - 1, n_gx)}

    core = lax.rem(gy, 2)

    def at(distance, z, on_core):
        return {"orb": lax.rem(ox + distance, 4) * 2 + z, "gy": gy - core + on_core}

    barrier = pltpu.get_barrier_semaphore()

    def signal(semaphore, device):
        pl.semaphore_signal(semaphore, inc=1, device_id=device, device_id_type=MESH)

    partners = [up, down, right, left]
    for to_core in (core, 1 - core):
        partners += [at(distance, oz, to_core) for distance in (2, 1, 3)]
    for partner in partners:
        signal(barrier, partner)

    @pl.when(oz == 0)
    def _():
        for to_core in range(2):
            signal(barrier, at(0, 1, to_core))
        signal(barrier, at(2, 1, core))

    loads = [
        pltpu.make_async_copy(
            orbitals.at[o], t0.at[:, o, pl.ds(TOP, ROWS)], local_sem.at[o]
        )
        for o in range(NORB)
    ]
    loads.append(pltpu.make_async_copy(potential, pot, local_sem.at[NORB]))
    loads.append(pltpu.make_async_copy(coeffs, small, local_sem.at[NORB + 1]))
    for load in loads:
        load.start()

    def y_copy(k, planes, position, way):
        term = terms[k]
        source, target = (TOP + ROWS - 4, TOP - 4) if way == 0 else (TOP, TOP + ROWS)
        return pltpu.make_async_remote_copy(
            src_ref=term.at[planes, :, pl.ds(source, 4)],
            dst_ref=term.at[planes, :, pl.ds(target, 4)],
            send_sem=y_send.at[k, way],
            recv_sem=y_recv.at[k, position, way],
            device_id=up if way == 0 else down,
            device_id_type=MESH,
        )

    def x_copy(k, position, way):
        return pltpu.make_async_remote_copy(
            src_ref=packed.at[k, position],
            dst_ref=beside.at[k, way, position],
            send_sem=x_send.at[k, way],
            recv_sem=x_recv.at[k, position, way],
            device_id=right if way == 0 else left,
            device_id_type=MESH,
        )

    def chunk_planes(position):
        return pl.ds(chunk_at(position) * PLANES, PLANES)

    def y_send_start(k, position):
        for way in range(2):
            y_copy(k, chunk_planes(position), position, way).start()

    def x_send_start(k, position):
        for way in range(2):
            x_copy(k, position, way).start()

    def send_edges(k, position):
        y_send_start(k, position)
        x_send_start(k, position)

    lane = lax.broadcasted_iota(jnp.int32, (ROWS, LANES), 1)
    in_left = lax.rem(lane, 8) < 4
    at_edge = (lane < 4) | (lane >= LANES - 4)

    group_of = lane // 8

    def pack(tiles):
        result = jnp.zeros((ROWS, LANES), jnp.float32)
        for g, tile in enumerate(tiles):
            result = jnp.where(group_of == g, pltpu.roll(tile, 8 * g + 4, 1), result)
        return result

    band[...] = band_weights()
    edge[...] = edge_weights()
    for load in loads:
        load.wait()

    @pl.loop(0, CHUNKS)
    def _(position):
        z = chunk_at(position) * PLANES
        packed[0, position] = pack(
            [t0[z + i, o, pl.ds(TOP, ROWS), :] for i in range(PLANES) for o in range(NORB)]
        )

    pl.semaphore_wait(barrier, len(partners) + 3 * oz)

    @pl.loop(0, CHUNKS)
    def _(position):
        send_edges(0, position)

    @pl.when(oz == 1)
    def _():
        signal(ready.at[0], at(0, 0, 1))

    @pl.loop(0, NZ // 4)
    def _(i):
        rows = pl.ds(i * 4, 4)
        pot[rows] = pot[rows] * (1.0 / SPREAD) + (-SHIFT / SPREAD + 3.0 * LAP[0])

    c0, c1, c2, c3 = small[0], small[1], small[2], small[3]

    def inside(k):
        term = terms[k]

        @pl.loop(0, NZ // SPAN)
        def _(span):
            z = span * SPAN
            block = [term[z + i, o, pl.ds(TOP, ROWS), :] for o in range(NORB) for i in range(SPAN)]
            along = MXU_SCALE * jnp.dot(
                split_bf16(jnp.concatenate(block, axis=0)),
                band[...],
                preferred_element_type=jnp.float32,
            )
            for o in range(NORB):
                for half in range(0, ROWS, 8):
                    rows = pl.ds(TOP + half, 8)
                    planes = [
                        term[lax.rem(z + d + NZ, NZ), o, rows, :] for d in range(-4, SPAN + 4)
                    ]
                    for i in range(SPAN):
                        first = (o * SPAN + i) * ROWS + half
                        centre = planes[4 + i]
                        total = pot[z + i, pl.ds(half, 8)] * centre + along[first : first + 8]
                        for j in range(1, 5):
                            total = total + LAP[j] * (planes[4 + i - j] + planes[4 + i + j])
                        if k == 0:
                            t1[z + i, o, rows, :] = total
                        elif k == 1:
                            t2[z + i, o, rows, :] = 2.0 * total - t0[z + i, o, rows, :]
                        else:
                            acc[z + i, o, pl.ds(half, 8)] = (
                                (2.0 * c3) * total
                                + c2 * centre
                                + (c1 - c3) * t1[z + i, o, rows, :]
                                + c0 * t0[z + i, o, rows, :]
                            )

    def side_terms(k, base):
        blocks = []
        for n in range(BATCH):
            for way in range(2):
                x_copy(k, base + n, way).wait_recv()
            blocks.append(
                jnp.where(in_left, beside[k, 0, base + n], beside[k, 1, base + n])
            )
        return MXU_SCALE * jnp.dot(
            split_bf16(jnp.concatenate(blocks, axis=0)),
            edge[...],
            preferred_element_type=jnp.float32,
        )

    def halo_terms(k, position, sides):
        term = terms[k]
        z = chunk_at(position) * PLANES
        totals = []
        for i in range(PLANES):
            for o in range(NORB):
                g = i * NORB + o
                total = jnp.where(at_edge, pltpu.roll(sides, LANES - 4 - 8 * g, 1), 0.0)
                for j in range(1, 5):
                    total = total + LAP[j] * (
                        term[z + i, o, pl.ds(TOP - j, ROWS), :]
                        + term[z + i, o, pl.ds(TOP + j, ROWS), :]
                    )
                totals.append(total)
        return z, totals

    def by_batches(k, finish, send):
        @pl.loop(0, CHUNKS // BATCH)
        def _(batch):
            base = batch * BATCH
            sides = side_terms(k, base)
            for first in range(0, BATCH, GROUP):
                group = range(first, first + GROUP)
                for n in group:
                    for way in range(2):
                        y_copy(k, chunk_planes(base + n), base + n, way).wait_recv()
                for n in group:
                    finish(base + n, *halo_terms(k, base + n, sides[ROWS * n : ROWS * (n + 1)]))
                for n in group:
                    send(base + n, n)

    for k in range(CHEB - 1):
        inside(k)

        def finish(position, z, totals, k=k):
            following = terms[k + 1]
            tiles = []
            for i in range(PLANES):
                for o in range(NORB):
                    total = totals[i * NORB + o]
                    if k > 0:
                        total = 2.0 * total
                    tile = following[z + i, o, pl.ds(TOP, ROWS), :] + total
                    following[z + i, o, pl.ds(TOP, ROWS), :] = tile
                    tiles.append(tile)
            y_send_start(k + 1, position)
            packed[k + 1, position] = pack(tiles)

        def send(position, n, k=k):
            x_send_start(k + 1, position)

        by_batches(k, finish, send)

    def q_copy(position):
        own = position // 4
        straight = jnp.where(position == 2, oz, 0)
        slot = jnp.where(straight == 1, 11, position + 4 * (own + core * (1 - own)))
        to_core = jnp.where(straight == 1, core, 1 - own * (1 - core))
        return pltpu.make_async_remote_copy(
            src_ref=squares.at[position],
            dst_ref=arrived.at[slot],
            send_sem=q_send.at[position],
            recv_sem=q_recv.at[slot],
            device_id=at(distance_at(position), oz - straight, to_core),
            device_id_type=MESH,
        )

    def wait_arrived(slots):
        for slot in slots:
            pltpu.make_async_copy(
                squares.at[0], arrived.at[slot], q_recv.at[slot]
            ).wait()

    def to_owner(on_core):
        return pltpu.make_async_remote_copy(
            src_ref=forward.at[on_core],
            dst_ref=other,
            send_sem=z_send.at[on_core],
            recv_sem=z_recv.at[0],
            device_id=at(0, 1 - oz, on_core),
            device_id_type=MESH,
        )

    inside(CHEB - 1)

    def finish(position, z, totals):
        for i in range(PLANES):
            total = None
            for o in range(NORB):
                value = acc[z + i, o] + (2.0 * c3) * totals[i * NORB + o]
                total = value * value if total is None else total + value * value
            squares[position, i] = total

    def send(position, n):
        @pl.when((position < 3) | ((position == 3) & (core == 0)))
        def _():
            q_copy(position).start()

    by_batches(CHEB - 1, finish, send)

    @pl.when(core == 1)
    def _():
        wait_arrived((4, 5))
        forward[1] = (squares[3] + arrived[4]) + arrived[5]

        @pl.when(oz == 0)
        def _():
            pl.semaphore_wait(ready.at[0], 2)
            wait_arrived((6,))
            forward[1] = forward[1] + arrived[6]

        to_owner(1).start()
        wait_arrived((0, 1, 3))
        forward[0] = (arrived[0] + arrived[1]) + arrived[3]

        @pl.when(oz == 0)
        def _():
            wait_arrived((2,))
            forward[0] = forward[0] + arrived[2]

        to_owner(0).start()

    for position in range(3):
        q_copy(position).wait_send()
    for position in range(4, 7):
        q_copy(position).start()

    for k in range(CHEB):
        for way in range(2):
            pltpu.make_async_remote_copy(
                src_ref=packed.at[k],
                dst_ref=beside.at[k, way],
                send_sem=x_send.at[k, way],
                recv_sem=x_recv.at[k, 0, way],
                device_id=right if way == 0 else left,
                device_id_type=MESH,
            ).wait_send()
            y_copy(k, pl.ds(0, NZ), 0, way).wait_send()
    for position in range(4, 7):
        q_copy(position).wait_send()

    @pl.when(core == 0)
    def _():
        q_copy(3).wait_send()

    wait_arrived((8, 9, 10))
    mine = (squares[7] + arrived[8]) + (arrived[9] + arrived[10])

    @pl.when(core == 1)
    def _():
        for on_core in range(2):
            to_owner(on_core).wait_send()

    to_owner(0).wait_recv()
    out[...] = mine + other[...]

    @pl.when(oz == 0)
    def _():
        wait_arrived((11,))
        out[...] = out[...] + arrived[11]


def local(orbitals, potential, coeffs):
    squares = pl.pallas_call(
        kernel,
        out_shape=jax.ShapeDtypeStruct((PLANES, ROWS, LANES), jnp.float32),
        in_specs=[
            pl.BlockSpec(memory_space=pl.ANY),
            pl.BlockSpec(memory_space=pl.ANY),
            pl.BlockSpec(memory_space=pl.ANY),
        ],
        out_specs=pl.BlockSpec(memory_space=pltpu.VMEM),
        scratch_shapes=[
            pltpu.VMEM((NZ, NORB, 32, LANES), jnp.float32),
            pltpu.VMEM((NZ, NORB, 32, LANES), jnp.float32),
            pltpu.VMEM((NZ, NORB, 32, LANES), jnp.float32),
            pltpu.VMEM((NZ, NORB, ROWS, LANES), jnp.float32),
            pltpu.VMEM((NZ, ROWS, LANES), jnp.float32),
            pltpu.VMEM((2 * LANES, LANES), jnp.bfloat16),
            pltpu.VMEM((2 * LANES, LANES), jnp.bfloat16),
            pltpu.VMEM((CHEB, CHUNKS, ROWS, LANES), jnp.float32),
            pltpu.VMEM((CHEB, 2, CHUNKS, ROWS, LANES), jnp.float32),
            pltpu.VMEM((CHUNKS, PLANES, ROWS, LANES), jnp.float32),
            pltpu.VMEM((12, PLANES, ROWS, LANES), jnp.float32),
            pltpu.VMEM((2, PLANES, ROWS, LANES), jnp.float32),
            pltpu.VMEM((PLANES, ROWS, LANES), jnp.float32),
            pltpu.SMEM((4,), jnp.float32),
            pltpu.SemaphoreType.DMA((NORB + 2,)),
            pltpu.SemaphoreType.DMA((CHEB, 2)),
            pltpu.SemaphoreType.DMA((CHEB, CHUNKS, 2)),
            pltpu.SemaphoreType.DMA((CHEB, 2)),
            pltpu.SemaphoreType.DMA((CHEB, CHUNKS, 2)),
            pltpu.SemaphoreType.DMA((CHUNKS,)),
            pltpu.SemaphoreType.DMA((12,)),
            pltpu.SemaphoreType.DMA((2,)),
            pltpu.SemaphoreType.DMA((1,)),
            pltpu.SemaphoreType.REGULAR((1,)),
        ],
        compiler_params=pltpu.CompilerParams(
            collective_id=0, has_side_effects=True, vmem_limit_bytes=48000 * 2**10
        ),
        name="chebyshev",
    )(*(pltpu.with_memory_space_constraint(a, pltpu.HBM) for a in (orbitals, potential, coeffs)))
    return squares * (1.0 / 16.0)


def solution(mesh):
    in_specs = (P("orb", None, "gy", "gx"), P(None, "gy", "gx"), P())
    out_specs = P("orb", "gy", "gx")
    return jax.shard_map(local, mesh=mesh, in_specs=in_specs, out_specs=out_specs, check_vma=False)
```
